32 devices in a mesh: ulysses: 4 (over z), dp: 8 (over y, x, core).
Axes of the slice: x: 2, y: 2, z: 4, core: 2. Of those that a mesh axis runs over, the one named last changes fastest.
Arguments:
- tokens: bfloat16 [8, 1024, 2048], P('dp', 'ulysses'), may hold values from -60 to 60
- d_out: bfloat16 [8, 1024, 2048], P('dp', 'ulysses'), may hold values from -6 to 6
- lengths: int32 [8, 10], P('dp'), may hold values from 1 to 384, 1024 in all within a row
- gain: bfloat16 [2048], P('dp'), may hold values from 0.5 to 1.5
- w_qkv: bfloat16 [2048, 1536], P('dp'), may hold values from -16 to 16
- w_out: bfloat16 [2048, 1024], P('dp'), may hold values from -0.1875 to 0.1875
Outputs:
- d_tokens: bfloat16 [8, 1024, 2048], P('dp', 'ulysses')
- d_w_qkv: float32 [2048, 1536], P(('ulysses', 'dp'))
- d_w_out: float32 [2048, 1024], P(('ulysses', 'dp'))
- d_gain: float32 [2048], P(('ulysses', 'dp'))
The draws below stay inside these ranges and needn't reach their ends.
Inputs may be any that keep to these rules, and one draw needn't show every extreme that they name: Each row holds whole document lengths of 1 to 384 tokens that sum to 1024; the longest is exactly 384.
All inputs are finite; a program needn't handle non-finite values.
Results may differ from the reference program's by a relative error of at most 0.01.
The reference program's roundings to bfloat16 on the way count: a program that leaves them out, or rounds other values in their place, can miss the bound.
Values may be sent and summed in bfloat16 or wider, within the bound.
No kernel may reach another device: no remote copies, remote signals or barrier semaphores. Data moves between devices by JAX's collectives and lax.ppermute only.
A program may use at most 128 MiB of HBM per device.

```python
import math
import jax
import jax.numpy as jnp
import numpy as np
from jax import lax

D = 2048
HEADS = 16
KV_HEADS = 4
HEAD_DIM = 64
DOC_MOST = 384
SEQ = 1024
GROUPS = 8
DOCS = 10
ALL_TOKENS = 8192
QW = 1024
KW = 256
QKVW = 1536
N_ULYSSES = 4


def draw_tokens(key, part):
    key_base, key_rows, key_cols = jax.random.split(key, 3)
    base = jax.random.normal(key_base, (GROUPS, SEQ, D), jnp.float32)
    row_scale = jnp.exp(jax.random.uniform(key_rows, (GROUPS, SEQ, 1), jnp.float32, 0.0, math.log(10.0)))
    col_scale = jnp.exp(jax.random.uniform(key_cols, (1, 1, D), jnp.float32, 0.0, math.log(10.0))) / 3.0
    return jnp.clip(base * row_scale * col_scale, -60.0, 60.0).astype(jnp.bfloat16)


def draw_w_qkv(key, part):
    key_base = jax.random.fold_in(key, 0)
    base = jnp.clip(jax.random.normal(key_base, (D, QKVW), jnp.float32), -6.0, 6.0) * D ** (-0.5)
    return jnp.clip(base, -16.0, 16.0).astype(jnp.bfloat16)


def levels(stream_key, dims, shards, least, high):
    def one(axis_at, shards_of):
        steps = jax.random.uniform(jax.random.fold_in(jax.random.fold_in(stream_key, 6), axis_at), (shards_of,), jnp.float32, least / len(shards), high / len(shards))
        return jnp.repeat(jnp.exp(steps), dims[axis_at] // shards_of).reshape((-1,) + (1,) * (len(dims) - axis_at - 1))

    loudness = one(*shards[0])
    for cut in shards[1:]:
        loudness = loudness * one(*cut)
    return loudness


def profile(amount, total, limit, slope):
    loads = [(1 << 20) // math.isqrt(standing ** slope) + 1 for standing in range(2, amount + 1)]
    surplus, holding = total - limit - (amount - 1), [1] * (amount - 1)
    while surplus > 0:
        free = [i for i in range(amount - 1) if holding[i] < limit]
        whole, left = sum([loads[i] for i in free]), surplus
        for i in free:
            addition = min(limit - holding[i], max(1, left * loads[i] // whole), surplus)
            holding[i] = holding[i] + addition
            surplus = surplus - addition
    return np.array([limit] + holding)


def uneven_parts(rng, number_of, total, most, slope):
    if number_of == 2:
        one = jax.random.randint(rng, (), max(1, total - most), min(most, total - 1) + 1)
        return jnp.stack([one, total - one])
    sizes = jnp.asarray(profile(number_of, total, most, slope), jnp.int32)
    pairs = (number_of - 1) // 2
    giver, receiver = sizes[1:1 + 2 * pairs:2], sizes[2:2 + 2 * pairs:2]
    margin = jnp.minimum(giver - 1, most - receiver)
    moved = jax.random.randint(jax.random.fold_in(rng, 1), (pairs,), 0, 1 << 20) % (margin + 1)
    sizes = sizes.at[1:1 + 2 * pairs:2].set(giver - moved).at[2:2 + 2 * pairs:2].set(receiver + moved)
    return sizes[jax.random.permutation(jax.random.fold_in(rng, 2), number_of)]


def noise(stream_key, shape, scale, most, shards=(), held_as=jnp.bfloat16):
    level = levels(stream_key, shape, shards, -0.22, 0.18) if shards else 1.0
    array = jax.random.normal(stream_key, shape, jnp.float32) * scale * level
    return jnp.minimum(jnp.maximum(array, -most), most).astype(held_as)


def setup_inputs(seed: int = 0) -> dict:
    key_list = jax.random.split(jax.random.key(seed), 7)
    return {
        "tokens": draw_tokens(jax.random.fold_in(key_list[6], 71), 0),
        "d_out": noise(key_list[1], (GROUPS, SEQ, D), 1.0, 6.0, ((0, 8), (1, 4))),
        "lengths": jax.vmap(lambda own: uneven_parts(own, DOCS, SEQ, DOC_MOST, 2))(jax.random.split(key_list[2], GROUPS)).reshape((GROUPS, DOCS)).astype(jnp.int32),
        "gain": jnp.clip(1.0 + 0.1 * jax.random.normal(key_list[3], (D,), jnp.float32), 0.5, 1.5).astype(jnp.bfloat16),
        "w_qkv": draw_w_qkv(jax.random.fold_in(key_list[6], 71), 0),
        "w_out": noise(key_list[5], (D, QW), QW ** -0.5, 0.1875, ((0, 8),)),
    }


EPS = 1e-05
ROPE_BASE = 500000.0

def doc_positions(doc_lengths, length):
    bounds = (jnp.cumsum(doc_lengths) - doc_lengths).astype(jnp.int32)
    places = jnp.arange(length, dtype=jnp.int32)
    begins = lax.optimization_barrier(jnp.max(jnp.where(bounds[None, :] <= places[:, None], bounds[None, :], 0), axis=1)).astype(jnp.int32)
    return (begins, (places - begins).astype(jnp.int32))

def rotary_tables(places):
    inverse = ROPE_BASE ** (-jnp.arange(0, HEAD_DIM, 2).astype(jnp.float32) / HEAD_DIM)
    angles = places.astype(jnp.float32)[:, None] * inverse[None, :]
    angles = jnp.concatenate([angles, angles], axis=1)
    return (jnp.cos(angles), jnp.sin(angles))

def rotate(values, cos_table, sin_table):
    half_dim = HEAD_DIM // 2
    turned = jnp.concatenate([-values[..., half_dim:], values[..., :half_dim]], axis=-1)
    return values * cos_table[:, None, :] + turned * sin_table[:, None, :]

def attend(query_head, key_head, value_head, grad_head, begins):
    length, heads_here, _ = query_head.shape
    block_len = min(512, length)
    blocks = length // block_len
    scale = HEAD_DIM ** (-0.5)
    filler = jnp.zeros((block_len, HEAD_DIM), key_head.dtype)
    key_blocks = jnp.concatenate([filler, key_head], axis=0).reshape(blocks + 1, block_len, HEAD_DIM)
    key_window = jnp.concatenate([key_blocks[:-1], key_blocks[1:]], axis=1)
    value_blocks = jnp.concatenate([filler, value_head], axis=0).reshape(blocks + 1, block_len, HEAD_DIM)
    value_window = jnp.concatenate([value_blocks[:-1], value_blocks[1:]], axis=1)
    query_blocks = query_head.reshape(blocks, block_len * heads_here, HEAD_DIM)
    grad_blocks = grad_head.reshape(blocks, block_len * heads_here, HEAD_DIM)
    begin_blocks = begins.reshape(blocks, block_len)

    def one_block(inputs):
        block_index, query_b, grad_b, key_w, value_w, begin_b = inputs
        query_pos = block_index * block_len + jnp.arange(block_len, dtype=jnp.int32)
        key_pos = (block_index - 1) * block_len + jnp.arange(2 * block_len, dtype=jnp.int32)
        allowed = (key_pos[None, :] >= begin_b[:, None]) & (key_pos[None, :] <= query_pos[:, None])
        allowed = jnp.broadcast_to(allowed[:, None, :], (block_len, heads_here, 2 * block_len))
        allowed = allowed.reshape(block_len * heads_here, 2 * block_len)
        scores = jnp.einsum('qd,kd->qk', query_b.astype(jnp.float32), key_w.astype(jnp.float32)) * scale
        scores = jnp.where(allowed, scores, -1e+30)
        peak = lax.optimization_barrier(jnp.max(scores, axis=1, keepdims=True))
        weights = jnp.where(allowed, jnp.exp(scores - peak), 0.0)
        shares = weights / lax.optimization_barrier(jnp.sum(weights, axis=1, keepdims=True))
        shares_low = shares.astype(jnp.bfloat16)
        mixed = jnp.dot(shares_low, value_w, preferred_element_type=jnp.float32)
        row_dot = lax.optimization_barrier(jnp.sum(grad_b.astype(jnp.float32) * mixed, axis=1, keepdims=True))
        d_shares = jnp.einsum('qd,kd->qk', grad_b.astype(jnp.float32), value_w.astype(jnp.float32))
        d_scores = (shares * (d_shares - row_dot) * scale).astype(jnp.bfloat16)
        d_query = jnp.dot(d_scores, key_w, preferred_element_type=jnp.float32)
        d_keys = jnp.einsum('qk,qd->kd', d_scores.astype(jnp.float32), query_b.astype(jnp.float32))
        d_values = jnp.einsum('qk,qd->kd', shares_low.astype(jnp.float32), grad_b.astype(jnp.float32))
        return (mixed.astype(jnp.bfloat16), d_query, d_keys, d_values)
    block_ids = jnp.arange(blocks, dtype=jnp.int32)
    mixed, d_query, d_keys, d_values = lax.map(one_block, (block_ids, query_blocks, grad_blocks, key_window, value_window, begin_blocks))
    mixed = mixed.reshape(length, heads_here * HEAD_DIM)
    d_query = d_query.reshape(length, heads_here, HEAD_DIM)
    pad_front = ((1, 0), (0, 0), (0, 0))
    pad_back = ((0, 1), (0, 0), (0, 0))
    d_keys = (jnp.pad(d_keys[:, :block_len], pad_back) + jnp.pad(d_keys[:, block_len:], pad_front))[1:]
    d_values = (jnp.pad(d_values[:, :block_len], pad_back) + jnp.pad(d_values[:, block_len:], pad_front))[1:]
    return (mixed, d_query, d_keys.reshape(length, HEAD_DIM), d_values.reshape(length, HEAD_DIM))

def head_side(head_block, begins, places, heads_here):
    length = head_block.shape[0]
    q_width = heads_here * HEAD_DIM
    query_head = head_block[:, :q_width].reshape(length, heads_here, HEAD_DIM)
    key_head = head_block[:, q_width:q_width + HEAD_DIM]
    value_head = head_block[:, q_width + HEAD_DIM:q_width + 2 * HEAD_DIM]
    grad_head = head_block[:, q_width + 2 * HEAD_DIM:].reshape(length, heads_here, HEAD_DIM)
    mixed, d_query, d_keys, d_values = attend(query_head, key_head, value_head, grad_head, begins)
    cos_table, sin_table = rotary_tables(places)
    d_query = rotate(d_query, cos_table, -sin_table).astype(jnp.bfloat16).reshape(length, q_width)
    d_keys = rotate(d_keys[:, None, :], cos_table, -sin_table)[:, 0, :].astype(jnp.bfloat16)
    d_values = d_values.astype(jnp.bfloat16)
    return jnp.concatenate([mixed, d_query, d_keys, d_values], axis=1)

def reference(tokens, d_out, lengths, gain, w_qkv, w_out):
    groups = N_ULYSSES
    heads_here = HEADS // groups
    repeat = groups // KV_HEADS
    q_width = heads_here * HEAD_DIM
    factor = 1.0 / math.sqrt(ALL_TOKENS)
    gain_wide = gain.astype(jnp.float32)

    def per_group(carry, inputs):
        token_rows, grad_rows, doc_lengths = inputs
        rows = token_rows.shape[0]
        begins, places = doc_positions(doc_lengths, rows)
        wide_rows = token_rows.astype(jnp.float32)
        inv_rms = lax.rsqrt(lax.optimization_barrier(jnp.mean(wide_rows * wide_rows, axis=1, keepdims=True)) + EPS)
        unit_rows = wide_rows * inv_rms
        normed = (unit_rows * gain_wide[None, :]).astype(jnp.bfloat16)
        projected = jnp.dot(normed, w_qkv, preferred_element_type=jnp.float32)
        cos_table, sin_table = rotary_tables(places)
        query = rotate(projected[:, :QW].reshape(rows, HEADS, HEAD_DIM), cos_table, sin_table).astype(jnp.bfloat16)
        key_rows = rotate(projected[:, QW:QW + KW].reshape(rows, KV_HEADS, HEAD_DIM), cos_table, sin_table).astype(jnp.bfloat16)
        value_rows = projected[:, QW + KW:].astype(jnp.bfloat16).reshape(rows, KV_HEADS, HEAD_DIM)
        key_rows = jnp.repeat(key_rows, repeat, axis=1)
        value_rows = jnp.repeat(value_rows, repeat, axis=1)
        d_attn = jnp.dot(grad_rows, w_out, preferred_element_type=jnp.float32).astype(jnp.bfloat16)
        packed = jnp.concatenate([query.reshape(rows, groups, q_width), key_rows, value_rows, d_attn.reshape(rows, groups, q_width)], axis=2)
        slots = jnp.transpose(packed, (1, 0, 2))
        outgoing = lax.map(lambda block: head_side(block, begins, places, heads_here), slots)
        returned = jnp.transpose(outgoing, (1, 0, 2))
        mixed_rows = returned[:, :, :q_width].reshape(rows, QW)
        dq_rows = returned[:, :, q_width:2 * q_width].reshape(rows, QW)
        dk_rows = returned[:, :, 2 * q_width:2 * q_width + HEAD_DIM].astype(jnp.float32)
        dk_rows = dk_rows.reshape(rows, KV_HEADS, repeat, HEAD_DIM).sum(axis=2).astype(jnp.bfloat16).reshape(rows, KW)
        dv_rows = returned[:, :, 2 * q_width + HEAD_DIM:].astype(jnp.float32)
        dv_rows = dv_rows.reshape(rows, KV_HEADS, repeat, HEAD_DIM).sum(axis=2).astype(jnp.bfloat16).reshape(rows, KW)
        d_proj = jnp.concatenate([dq_rows, dk_rows, dv_rows], axis=1)
        grad_qkv = jnp.einsum('td,tc->dc', normed.astype(jnp.float32), d_proj.astype(jnp.float32))
        grad_out = jnp.einsum('td,tc->dc', grad_rows.astype(jnp.float32), mixed_rows.astype(jnp.float32))
        d_normed = jnp.einsum('tc,dc->td', d_proj.astype(jnp.float32), w_qkv.astype(jnp.float32))
        grad_gain = lax.optimization_barrier(jnp.sum(d_normed * unit_rows, axis=0))
        scaled = d_normed * gain_wide[None, :]
        d_rows = inv_rms * (scaled - unit_rows * lax.optimization_barrier(jnp.mean(scaled * unit_rows, axis=1, keepdims=True)))
        d_tokens = (grad_rows.astype(jnp.float32) + d_rows).astype(jnp.bfloat16)
        return ((carry[0] + grad_qkv, carry[1] + grad_out, carry[2] + grad_gain), d_tokens)
    start = (jnp.zeros((D, QKVW), jnp.float32), jnp.zeros((D, QW), jnp.float32), jnp.zeros((D,), jnp.float32))
    summed, d_tokens = lax.scan(per_group, start, (tokens, d_out, lengths))
    return (d_tokens, summed[0] * factor, summed[1] * factor, summed[2] * factor)
```

```python
import functools
import math

import jax
import jax.numpy as jnp
from jax import lax
from jax.experimental import pallas as pl
from jax.experimental.pallas import tpu as pltpu
from jax.sharding import PartitionSpec as P

HEADS = 16
KV_HEADS = 4
HEAD_DIM = 64
QW = 1024
KW = 256
DOC_MOST = 384
Q_BLOCK = 128

EPS = 1e-05
ROPE_BASE = 500000.0
SCALE = HEAD_DIM ** (-0.5)

bf16 = jnp.bfloat16
f32 = jnp.float32


def params(mib):
    return pltpu.CompilerParams(vmem_limit_bytes=mib << 20)


SMEM = pl.BlockSpec(memory_space=pltpu.SMEM)
VMEM = pl.BlockSpec(memory_space=pltpu.VMEM)


def nt(a, b):
    return lax.dot_general(a, b, (((1,), (1,)), ((), ())), preferred_element_type=f32)


def tn(a, b):
    return lax.dot_general(a, b, (((0,), (0,)), ((), ())), preferred_element_type=f32)


def nn(a, b):
    return jnp.dot(a, b, preferred_element_type=f32)


def swap(a, axis, bit):
    n = lax.axis_size(axis)
    return lax.ppermute(a, axis, [(i, i ^ bit) for i in range(n)])


def gather_slots(a, axis, split):
    n = lax.axis_size(axis)
    slots = {0: [a]}
    if n >= 4:
        first, second = n // 4, n // 2
        over_first, over_second = swap(a, axis, first), swap(a, axis, second)
        upper = swap(over_first[:split], axis, second)
        lower = swap(over_second[split:], axis, first)
        slots[first], slots[second] = [over_first], [over_second]
        slots[first | second] = [upper, lower]
        bit = n // 8
    else:
        bit = n // 2
    while bit >= 1:
        for j in list(slots):
            slots[j ^ bit] = [swap(piece, axis, bit) for piece in slots[j]]
        bit //= 2
    return [slots[j] for j in range(n)]


def flat(slots):
    return [piece for slot in slots for piece in slot], [len(slot) for slot in slots]


def regroup(refs, counts):
    out, at = [], 0
    for c in counts:
        out.append(refs[at : at + c])
        at += c
    return out


def whole_slot(pieces, rows):
    values = [p[...] for p in pieces]
    value = values[0] if len(values) == 1 else jnp.concatenate(values, axis=0)
    return value[:rows], value


def turn(x, lower):
    return jnp.where(lower, pltpu.roll(x, 96, 1), pltpu.roll(x, 32, 1))


def lower_lanes(rows):
    return lax.broadcasted_iota(jnp.int32, (rows, 128), 1) % HEAD_DIM < HEAD_DIM // 2


def inverse_rms(x):
    return lax.rsqrt(jnp.mean(x * x, axis=1, keepdims=True) + EPS)


def proj_kernel(counts, groups, me_ref, tok_ref, cos_ref, sin_ref, *refs):
    n = len(counts)
    slots = regroup(refs[: sum(counts)], counts)
    outs = refs[sum(counts) : sum(counts) + groups]
    normed_ref, acc = refs[sum(counts) + groups :]
    u, d = me_ref[0], me_ref[1]
    rows, width = tok_ref.shape
    part = width // n
    inv = inverse_rms(tok_ref[...].astype(f32))
    for j in range(n):
        at = pl.multiple_of((d ^ j) * part, part)
        w, ext = whole_slot(slots[j], part)
        gain = ext[part : part + 1, :part].astype(f32)
        normed = (tok_ref[:, pl.ds(at, part)].astype(f32) * inv * gain).astype(bf16)
        normed_ref[:, pl.ds(at, part)] = normed
        term = nn(normed, w)
        if j == 0:
            acc[...] = term
        else:
            acc[...] += term
    lower = lower_lanes(rows)
    cos, sin = cos_ref[...], sin_ref[...]
    turned = []
    for c in range((QW + KW) // 128):
        x = acc[:, c * 128 : (c + 1) * 128]
        turned.append((x * cos + turn(x, lower) * sin).astype(bf16))
    heads = HEADS // groups
    repeat = groups // KV_HEADS
    for g in range(groups):
        qw = heads * HEAD_DIM
        q = jnp.concatenate(turned[g * qw // 128 : (g + 1) * qw // 128], axis=1)
        kh = g // repeat
        at = QW // 128 + kh // 2
        half = (kh % 2) * HEAD_DIM
        k = turned[at][:, half : half + HEAD_DIM]
        v = acc[:, QW + KW + kh * HEAD_DIM : QW + KW + (kh + 1) * HEAD_DIM].astype(bf16)
        piece = jnp.concatenate([q, k, v], axis=1)
        for j in range(groups):

            @pl.when((u ^ g) == j)
            def _():
                outs[j][...] = piece


def d_attn_kernel(counts, groups, me_ref, d_out_ref, *refs):
    n = len(counts)
    slots = regroup(refs[: sum(counts)], counts)
    outs = refs[sum(counts) : sum(counts) + groups]
    acc = refs[-1]
    u, d = me_ref[0], me_ref[1]
    part = d_out_ref.shape[1] // n
    for j in range(n):
        at = pl.multiple_of((d ^ j) * part, part)
        w, _ = whole_slot(slots[j], part)
        term = nn(d_out_ref[:, pl.ds(at, part)], w)
        if j == 0:
            acc[...] = term
        else:
            acc[...] += term
    qw = QW // groups
    for g in range(groups):
        piece = acc[:, g * qw : (g + 1) * qw].astype(bf16)
        for j in range(groups):

            @pl.when((u ^ g) == j)
            def _():
                outs[j][...] = piece


def slices_kernel(n, groups, me_ref, normed_ref, d_out_ref, *refs):
    outs = refs[:n]
    turned = refs[n]
    d = me_ref[1]
    width = normed_ref.shape[1]
    block = width // (groups * n)
    for side, ref in enumerate((normed_ref, d_out_ref)):
        turned[...] = ref[...].T
        for j in range(n):
            for g in range(groups):
                at = pl.multiple_of(g * (width // groups) + (d ^ j) * block, block)
                outs[j][pl.ds((side * groups + g) * block, block), :] = turned[pl.ds(at, block), :]


def attend_kernel(groups, me_ref, begin_ref, cos_ref, sin_ref, *refs):
    qkv_refs, grad_refs = refs[:groups], refs[groups : 2 * groups]
    attn_outs, back_outs = refs[2 * groups : 3 * groups], refs[3 * groups : 4 * groups]
    q_all, kv_all, g_all, attn_all, dq_all, dkv_all, acc, p_low, s_low = refs[4 * groups :]
    u = me_ref[0]
    length, qw = q_all.shape
    heads = qw // HEAD_DIM
    rows = length // groups
    for j in range(groups):
        at = pl.ds(pl.multiple_of((u ^ j) * rows, rows), rows)
        q_all[at, :] = qkv_refs[j][:, :qw] * jnp.asarray(SCALE, bf16)
        kv_all[at, :] = qkv_refs[j][:, qw:]
        g_all[at, :] = grad_refs[j][...]
    acc[...] = jnp.zeros_like(acc)
    for b in range(length // Q_BLOCK):
        q0 = b * Q_BLOCK
        w0 = max(0, q0 - DOC_MOST)
        w1 = q0 + Q_BLOCK
        win = w1 - w0
        here = slice(q0, w1)
        keys = kv_all[w0:w1, :HEAD_DIM]
        values = kv_all[w0:w1, HEAD_DIM:]
        key_pos = w0 + lax.broadcasted_iota(jnp.int32, (Q_BLOCK, win), 1)
        row_pos = q0 + lax.broadcasted_iota(jnp.int32, (Q_BLOCK, win), 0)
        allowed = (key_pos >= begin_ref[here, :]) & (key_pos <= row_pos)
        bias = jnp.where(allowed, 0.0, -1e30).astype(f32)
        queries, grads, mixes, d_queries = [], [], [], []
        for h in range(heads):
            lanes = slice(h * HEAD_DIM, (h + 1) * HEAD_DIM)
            query, grad = q_all[here, lanes], g_all[here, lanes]
            scores = nt(query, keys) + bias
            peak = jnp.max(scores, axis=1, keepdims=True)
            weights = jnp.exp(scores - peak)
            shares = weights * (1.0 / jnp.sum(weights, axis=1, keepdims=True))
            shares_low = shares.astype(bf16)
            mixed = nn(shares_low, values)
            row_dot = jnp.sum(grad.astype(f32) * mixed, axis=1, keepdims=True)
            d_scores = (shares * (nt(grad, values) - row_dot)).astype(bf16)
            d_queries.append(nn(d_scores, keys) * SCALE)
            mixes.append(mixed)
            p_low[h * Q_BLOCK : (h + 1) * Q_BLOCK, :win] = shares_low
            s_low[h * Q_BLOCK : (h + 1) * Q_BLOCK, :win] = d_scores
            queries.append(query)
            grads.append(grad)
        attn_all[here, :] = jnp.concatenate(mixes, axis=1).astype(bf16)
        dq_all[here, :] = jnp.concatenate(d_queries, axis=1)
        acc[:HEAD_DIM, w0:w1] += tn(jnp.concatenate(queries, axis=0), s_low[:, :win])
        acc[HEAD_DIM:, w0:w1] += tn(jnp.concatenate(grads, axis=0), p_low[:, :win])
    dkv_all[...] = acc[...].T
    lower = lower_lanes(rows)
    value_lane = lax.broadcasted_iota(jnp.int32, (rows, 128), 1) >= HEAD_DIM
    for g in range(groups):
        here = slice(g * rows, (g + 1) * rows)
        cos, sin = cos_ref[here, :], sin_ref[here, :]
        parts = []
        for c in range(qw // 128):
            x = dq_all[here, c * 128 : (c + 1) * 128]
            parts.append(x * cos - turn(x, lower) * sin)
        x = dkv_all[here, :]
        parts.append(jnp.where(value_lane, x, x * cos - turn(x, lower) * sin))
        back = jnp.concatenate(parts, axis=1).astype(bf16)
        mixed = attn_all[here, :]
        for j in range(groups):

            @pl.when((u ^ g) == j)
            def _():
                attn_outs[j][...] = mixed
                back_outs[j][...] = back


def join_attn_kernel(groups, me_ref, *refs):
    u, out = me_ref[0], refs[groups]
    qw = QW // groups
    for j in range(groups):
        at = pl.multiple_of((u ^ j) * qw, qw)
        out[:, pl.ds(at, qw)] = refs[j][...]


def join_proj_kernel(groups, me_ref, *refs):
    u, out = me_ref[0], refs[groups]
    wide = refs[groups + 1]
    qw = QW // groups
    repeat = groups // KV_HEADS
    wide[...] = jnp.zeros_like(wide)
    for j in range(groups):
        at = pl.multiple_of((u ^ j) * qw, qw)
        out[:, pl.ds(at, qw)] = refs[j][:, :qw]
        back = refs[j][:, qw:].astype(f32)
        for kh in range(KV_HEADS):

            @pl.when((u ^ j) // repeat == kh)
            def _():
                wide[:, kh * 128 : (kh + 1) * 128] += back

    low = wide[...].astype(bf16)
    for at, half in ((QW, 0), (QW + KW, HEAD_DIM)):
        heads = [low[:, kh * 128 + half : kh * 128 + half + HEAD_DIM] for kh in range(KV_HEADS)]
        out[:, at : at + KW] = jnp.concatenate(heads, axis=1)


def tokens_kernel(counts, groups, factor, me_ref, tok_ref, d_out_ref, d_proj_ref, *refs):
    n = len(counts)
    slots = regroup(refs[: sum(counts)], counts)
    d_tok_ref, d_gain_ref, wide, gains = refs[sum(counts) :]
    d = me_ref[1]
    width = tok_ref.shape[1]
    part = width // n
    d_proj = d_proj_ref[...]
    for j in range(n):
        at = pl.multiple_of((d ^ j) * part, part)
        w, ext = whole_slot(slots[j], part)
        wide[:, pl.ds(at, part)] = nt(d_proj, w)
        gains[:, pl.ds(at, part)] = ext[part : part + 1, :part].astype(f32)
    x = tok_ref[...].astype(f32)
    inv = inverse_rms(x)
    unit = x * inv
    d_normed = wide[...]
    d_gain = jnp.sum(d_normed * unit, axis=0, keepdims=True) * factor
    scaled = d_normed * gains[...]
    mean = jnp.mean(scaled * unit, axis=1, keepdims=True)
    d_tok_ref[...] = (d_out_ref[...].astype(f32) + inv * (scaled - unit * mean)).astype(bf16)
    block = width // (groups * n)
    for e in range(n):
        starts = [g * (width // groups) + e * block for g in range(groups)]
        mine = jnp.concatenate([d_gain[:, s : s + block] for s in starts], axis=1)
        d_gain_ref[pl.ds(d ^ e, 1)] = mine[None]


def grads_kernel(counts, side, groups, factor, has_gain, *refs):
    n = len(counts)
    slices = refs[:n]
    slots = regroup(refs[n : n + sum(counts)], counts)
    rest = refs[n + sum(counts) :]
    gains, (out, acc) = (rest[:n], rest[n:]) if has_gain else ((), rest)
    kept = acc.shape[0]
    for j in range(n):
        a = slices[j][side * kept : (side + 1) * kept, :]
        b, _ = whole_slot(slots[j], a.shape[1])
        term = nn(a, b)
        if j == 0:
            acc[...] = term
        else:
            acc[...] += term
    block = kept // groups
    for g in range(groups):
        out[g, :block, :] = acc[g * block : (g + 1) * block, :] * factor
    if has_gain:
        total = gains[0][0]
        for j in range(1, n):
            total = total + gains[j][0]
        for g in range(groups):
            out[g, block:, :] = jnp.zeros_like(out[g, block:, :])
            out[g, block : block + 1, :block] = total[:, g * block : (g + 1) * block]


def chain_sum(local, axis):
    n = lax.axis_size(axis)
    me = lax.axis_index(axis)

    def block(at):
        return lax.dynamic_index_in_dim(local, jnp.clip(at, 0, n - 1), 0, keepdims=False)

    up = down = None
    for step in range(n - 1):
        a, b = block(n - 1 - step + me), block(me - (n - 1) + step)
        up = a if up is None else a + up
        down = b if down is None else b + down
        up = lax.ppermute(up, axis, [(i, i + 1) for i in range(step + 1)])
        down = lax.ppermute(down, axis, [(n - 1 - i, n - 2 - i) for i in range(step + 1)])
    return block(me) + up + down


def shape(*dims, dtype=bf16):
    return jax.ShapeDtypeStruct(dims, dtype)


def body(tokens, d_out, lengths, gain, w_qkv, w_out):
    groups, n = lax.axis_size("ulysses"), lax.axis_size("dp")
    u, d = lax.axis_index("ulysses"), lax.axis_index("dp")
    me = jnp.stack([u, d]).astype(jnp.int32)
    token_rows, grad_rows = tokens[0], d_out[0]
    rows, width = token_rows.shape
    length = rows * groups
    part = width // n
    heads = HEADS // groups
    qw = heads * HEAD_DIM
    columns = w_qkv.shape[1]
    factor = 1.0 / math.sqrt(length * n)
    block = width // (groups * n)
    kept = block * groups

    gain_rows = jnp.pad(gain[None, :], ((0, 15), (0, columns - part)))
    qkv_slots = gather_slots(jnp.concatenate([w_qkv, gain_rows], axis=0), "dp", part // 2)
    out_slots = gather_slots(w_out, "dp", part // 2)
    qkv_flat, qkv_counts = flat(qkv_slots)
    out_flat, out_counts = flat(out_slots)

    bounds = jnp.cumsum(lengths[0]) - lengths[0]
    places = jnp.arange(length, dtype=jnp.int32)
    begins = jnp.max(jnp.where(bounds[None, :] <= places[:, None], bounds[None, :], 0), axis=1)
    places = places - begins
    inverse = ROPE_BASE ** (-jnp.arange(0, HEAD_DIM, 2).astype(f32) / HEAD_DIM)
    angles = places.astype(f32)[:, None] * jnp.tile(inverse, 4)[None, :]
    signs = jnp.where(jnp.arange(128) % HEAD_DIM < HEAD_DIM // 2, -1.0, 1.0).astype(f32)
    cos, sin = jnp.cos(angles), jnp.sin(angles) * signs[None, :]
    cos_here = lax.dynamic_slice_in_dim(cos, u * rows, rows)
    sin_here = lax.dynamic_slice_in_dim(sin, u * rows, rows)

    *pieces, normed = pl.pallas_call(
        functools.partial(proj_kernel, qkv_counts, groups),
        out_shape=[shape(rows, qw + 128)] * groups + [shape(rows, width)],
        in_specs=[SMEM] + [VMEM] * (3 + len(qkv_flat)),
        out_specs=[VMEM] * (groups + 1),
        scratch_shapes=[pltpu.VMEM((rows, columns), f32)],
        compiler_params=params(32),
        name="proj",
    )(me, token_rows, cos_here, sin_here, *qkv_flat)
    qkv_here = [pieces[0]] + [swap(pieces[j], "ulysses", j) for j in range(1, groups)]

    pieces = pl.pallas_call(
        functools.partial(d_attn_kernel, out_counts, groups),
        out_shape=[shape(rows, qw)] * groups,
        in_specs=[SMEM] + [VMEM] * (1 + len(out_flat)),
        out_specs=[VMEM] * groups,
        scratch_shapes=[pltpu.VMEM((rows, QW), f32)],
        compiler_params=params(32),
        name="d_attn",
    )(me, grad_rows, *out_flat)
    grads_here = [pieces[0]] + [swap(pieces[j], "ulysses", j) for j in range(1, groups)]

    slices = pl.pallas_call(
        functools.partial(slices_kernel, n, groups),
        out_shape=[shape(2 * kept, rows)] * n,
        in_specs=[SMEM] + [VMEM] * 2,
        out_specs=[VMEM] * n,
        scratch_shapes=[pltpu.VMEM((width, rows), bf16)],
        compiler_params=params(32),
        name="slices",
    )(me, normed, grad_rows)
    slices = [slices[0]] + [swap(slices[j], "dp", j) for j in range(1, n)]

    outs = pl.pallas_call(
        functools.partial(attend_kernel, groups),
        out_shape=[shape(rows, qw)] * groups + [shape(rows, qw + 128)] * groups,
        in_specs=[SMEM] + [VMEM] * (3 + 2 * groups),
        out_specs=[VMEM] * (2 * groups),
        scratch_shapes=[
            pltpu.VMEM((length, qw), bf16),
            pltpu.VMEM((length, 128), bf16),
            pltpu.VMEM((length, qw), bf16),
            pltpu.VMEM((length, qw), bf16),
            pltpu.VMEM((length, qw), f32),
            pltpu.VMEM((length, 128), f32),
            pltpu.VMEM((128, length), f32),
            pltpu.VMEM((heads * Q_BLOCK, DOC_MOST + Q_BLOCK), bf16),
            pltpu.VMEM((heads * Q_BLOCK, DOC_MOST + Q_BLOCK), bf16),
        ],
        compiler_params=params(40),
        name="attend",
    )(me, begins[:, None], cos, sin, *qkv_here, *grads_here)
    mixed, back = outs[:groups], outs[groups:]
    mixed = [mixed[0]] + [swap(mixed[j], "ulysses", j) for j in range(1, groups)]
    back = [back[0]] + [swap(back[j], "ulysses", j) for j in range(1, groups)]

    attn = pl.pallas_call(
        functools.partial(join_attn_kernel, groups),
        out_shape=shape(rows, QW),
        in_specs=[SMEM] + [VMEM] * groups,
        out_specs=VMEM,
        name="join_attn",
    )(me, *mixed)
    attn_flat, attn_counts = flat(gather_slots(attn, "dp", rows // 2))

    d_proj = pl.pallas_call(
        functools.partial(join_proj_kernel, groups),
        out_shape=shape(rows, columns),
        in_specs=[SMEM] + [VMEM] * groups,
        out_specs=VMEM,
        scratch_shapes=[pltpu.VMEM((rows, 128 * KV_HEADS), f32)],
        name="join_proj",
    )(me, *back)
    proj_flat, proj_counts = flat(gather_slots(d_proj, "dp", rows // 2))

    d_tokens, d_gain = pl.pallas_call(
        functools.partial(tokens_kernel, qkv_counts, groups, factor),
        out_shape=[shape(rows, width), shape(n, 1, kept, dtype=f32)],
        in_specs=[SMEM] + [VMEM] * (3 + len(qkv_flat)),
        out_specs=[VMEM] * 2,
        scratch_shapes=[pltpu.VMEM((rows, width), f32), pltpu.VMEM((1, width), f32)],
        compiler_params=params(40),
        name="d_tokens",
    )(me, token_rows, grad_rows, d_proj, *qkv_flat)
    gains = [d_gain[:1]] + [swap(d_gain[j : j + 1], "dp", j) for j in range(1, n)]

    d_w_out = pl.pallas_call(
        functools.partial(grads_kernel, attn_counts, 1, groups, factor, False),
        out_shape=shape(groups, block, QW, dtype=f32),
        in_specs=[VMEM] * (n + len(attn_flat)),
        out_specs=VMEM,
        scratch_shapes=[pltpu.VMEM((kept, QW), f32)],
        compiler_params=params(32),
        name="d_w_out",
    )(*slices, *attn_flat)
    d_w_out = chain_sum(d_w_out, "ulysses")

    d_w_qkv = pl.pallas_call(
        functools.partial(grads_kernel, proj_counts, 0, groups, factor, True),
        out_shape=shape(groups, block + 8, columns, dtype=f32),
        in_specs=[VMEM] * (n + len(proj_flat) + n),
        out_specs=VMEM,
        scratch_shapes=[pltpu.VMEM((kept, columns), f32)],
        compiler_params=params(32),
        name="d_w_qkv",
    )(*slices, *proj_flat, *gains)
    summed = chain_sum(d_w_qkv, "ulysses")
    return (d_tokens[None], summed[:block], d_w_out, summed[block, :block])


def solution(mesh):
    in_specs = (
        P("dp", "ulysses", None),
        P("dp", "ulysses", None),
        P("dp", None),
        P("dp"),
        P("dp", None),
        P("dp", None),
    )
    out_specs = (
        P("dp", "ulysses", None),
        P(("ulysses", "dp"), None),
        P(("ulysses", "dp"), None),
        P(("ulysses", "dp")),
    )
    return jax.shard_map(body, mesh=mesh, in_specs=in_specs, out_specs=out_specs, check_vma=False)
```

```python
import functools
import math

import jax
import jax.numpy as jnp
from jax import lax
from jax.experimental import pallas as pl
from jax.experimental.pallas import tpu as pltpu
from jax.sharding import PartitionSpec as P

HEADS = 16
KV_HEADS = 4
HEAD_DIM = 64
QW = 1024
KW = 256
DOC_MOST = 384
Q_BLOCK = 128

EPS = 1e-05
ROPE_BASE = 500000.0
SCALE = HEAD_DIM ** (-0.5)

bf16 = jnp.bfloat16
f32 = jnp.float32


def params(mib):
    return pltpu.CompilerParams(vmem_limit_bytes=mib << 20)


def about(us):
    return pl.CostEstimate(flops=int(us * 1e9), bytes_accessed=int(us * 3e6), transcendentals=0)


SMEM = pl.BlockSpec(memory_space=pltpu.SMEM)
VMEM = pl.BlockSpec(memory_space=pltpu.VMEM)
ANY = pl.BlockSpec(memory_space=pl.ANY)


def nt(a, b):
    return lax.dot_general(a, b, (((1,), (1,)), ((), ())), preferred_element_type=f32)


def tn(a, b):
    return lax.dot_general(a, b, (((0,), (0,)), ((), ())), preferred_element_type=f32)


def nn(a, b):
    return jnp.dot(a, b, preferred_element_type=f32)


def swap(a, axis, bit):
    n = lax.axis_size(axis)
    return lax.ppermute(a, axis, [(i, i ^ bit) for i in range(n)])


def neighbours(a, axis):
    n = lax.axis_size(axis)
    return swap(a, axis, n // 4), swap(a, axis, n // 2)


def relay(own, first, second, *earlier):
    rows, columns = own.shape
    half = rows // 32 * 16

    def kernel(own_ref, first_ref, second_ref, *refs):
        upper, lower, trio = refs[-3:]
        upper[...] = first_ref[:half, :]
        lower[...] = second_ref[half:, :]
        trio[:rows, :] = own_ref[...]
        trio[rows : 2 * rows, :] = first_ref[...]
        trio[2 * rows :, :] = second_ref[...]

    return pl.pallas_call(
        kernel,
        out_shape=[shape(half, columns), shape(rows - half, columns), shape(3 * rows, columns)],
        in_specs=[VMEM] * 3 + [ANY] * len(earlier),
        out_specs=[VMEM] * 3,
        compiler_params=params(56),
        cost_estimate=about(2),
        name="relay",
    )(own, first, second, *earlier)


def complete(upper, lower, trio, axis):
    n = lax.axis_size(axis)
    rows, half = trio.shape[0] // 3, upper.shape[0]
    upper, lower = swap(upper, axis, n // 2), swap(lower, axis, n // 4)
    arrays = [trio, upper, lower]
    slots = {
        0: [(0, 0, rows)],
        n // 4: [(0, rows, rows)],
        n // 2: [(0, 2 * rows, rows)],
        n // 4 | n // 2: [(1, 0, half), (2, 0, rows - half)],
    }
    bit = n // 8
    while bit >= 1:
        at = len(arrays)
        arrays += [swap(a, axis, bit) for a in arrays]
        for j in list(slots):
            slots[j ^ bit] = [(i + at, start, size) for i, start, size in slots[j]]
        bit //= 2
    return arrays, [slots[j] for j in range(n)]


def whole_slot(refs, pieces, rows):
    values = [refs[i][start : start + size, :] for i, start, size in pieces]
    value = values[0] if len(values) == 1 else jnp.concatenate(values, axis=0)
    return value[:rows], value


def turn(x, lower):
    return jnp.where(lower, pltpu.roll(x, 96, 1), pltpu.roll(x, 32, 1))


def lower_lanes(rows):
    return lax.broadcasted_iota(jnp.int32, (rows, 128), 1) % HEAD_DIM < HEAD_DIM // 2


def inverse_rms(x):
    return lax.rsqrt(jnp.mean(x * x, axis=1, keepdims=True) + EPS)


def proj_kernel(slots, many, groups, me_ref, tok_ref, cos_ref, sin_ref, *refs):
    n = len(slots)
    outs, (normed_ref, acc) = refs[-groups - 2 : -2], refs[-2:]
    u, d = me_ref[0], me_ref[1]
    rows, width = tok_ref.shape
    part = width // n
    inv = inverse_rms(tok_ref[...].astype(f32))
    for j in range(n):
        at = pl.multiple_of((d ^ j) * part, part)
        w, ext = whole_slot(refs, slots[j], part)
        gain = ext[part : part + 1, :part].astype(f32)
        normed = (tok_ref[:, pl.ds(at, part)].astype(f32) * inv * gain).astype(bf16)
        normed_ref[:, pl.ds(at, part)] = normed
        term = nn(normed, w[:, : acc.shape[1]])
        if j == 0:
            acc[...] = term
        else:
            acc[...] += term
    lower = lower_lanes(rows)
    cos, sin = cos_ref[...], sin_ref[...]
    turned = []
    for c in range((QW + KW) // 128):
        x = acc[:, c * 128 : (c + 1) * 128]
        turned.append((x * cos + turn(x, lower) * sin).astype(bf16))
    heads = HEADS // groups
    repeat = groups // KV_HEADS
    for g in range(groups):
        qw = heads * HEAD_DIM
        q = jnp.concatenate(turned[g * qw // 128 : (g + 1) * qw // 128], axis=1)
        kh = g // repeat
        at = QW // 128 + kh // 2
        half = (kh % 2) * HEAD_DIM
        k = turned[at][:, half : half + HEAD_DIM]
        v = acc[:, QW + KW + kh * HEAD_DIM : QW + KW + (kh + 1) * HEAD_DIM].astype(bf16)
        piece = jnp.concatenate([q, k, v], axis=1)
        for j in range(groups):

            @pl.when((u ^ g) == j)
            def _():
                outs[j][...] = piece


def spread(own, axis):
    n = lax.axis_size(axis)
    slots = {0: own}
    far = 1
    while far < n:
        slots[far] = swap(own, axis, far)
        for j in range(1, (far + 1) // 2):
            slots[far ^ j] = swap(slots[far], axis, j)
        far = 2 * far + 1
    return [slots[j] for j in range(n)]


def d_attn_kernel(slots, groups, columns, me_ref, *refs):
    shards, arrays = refs[: 2 * groups], refs[2 * groups :]
    out, weight = refs[-2:]
    u, d = me_ref[0], me_ref[1]
    n = len(slots)
    rows, width = shards[0].shape
    part = width // n
    for j in range(n):
        at = pl.multiple_of((d ^ j) * part, part)
        weight[pl.ds(at, part), :] = whole_slot(arrays, slots[j], part)[0][:, columns:]
    for side in range(2):
        for j in range(groups):
            at = pl.multiple_of((2 * (u ^ j) + side) * rows, rows)
            out[pl.ds(at, rows), :] = nn(shards[side * groups + j][...], weight[...]).astype(bf16)


def slices_kernel(n, groups, normed_ref, d_out_ref, *refs):
    out, turned = refs[-2:]
    width = normed_ref.shape[1]
    block = width // (groups * n)
    for side, ref in enumerate((normed_ref, d_out_ref)):
        turned[...] = ref[...].T
        for e in range(n):
            for g in range(groups):
                at = g * (width // groups) + e * block
                to = (side * groups + g) * block
                out[e, to : to + block, :] = turned[at : at + block, :]


def collect(u, pieces, *wholes):
    rows = pieces[0].shape[0]
    for j, piece in enumerate(pieces):
        at = pl.ds(pl.multiple_of((u ^ j) * rows, rows), rows)
        lane = 0
        for whole, scale in wholes:
            part = piece[:, lane : lane + whole.shape[1]]
            whole[at, :] = part if scale is None else part * jnp.asarray(scale, bf16)
            lane += whole.shape[1]


def hand_out(u, g, value, outs):
    for j, out in enumerate(outs):

        @pl.when((u ^ g) == j)
        def _():
            out[...] = value


def doc_starts(lengths_ref):
    starts = [jnp.int32(0)]
    for i in range(lengths_ref.shape[0] - 1):
        starts.append(starts[-1] + lengths_ref[i])
    return starts


def window(b, starts):
    q0 = b * Q_BLOCK
    w0, w1 = max(0, q0 - DOC_MOST), q0 + Q_BLOCK
    key_pos = w0 + lax.broadcasted_iota(jnp.int32, (Q_BLOCK, w1 - w0), 1)
    row_pos = q0 + lax.broadcasted_iota(jnp.int32, (Q_BLOCK, w1 - w0), 0)
    row_at = q0 + lax.broadcasted_iota(jnp.int32, (Q_BLOCK, 1), 0)
    begin = jnp.zeros((Q_BLOCK, 1), jnp.int32)
    for start in starts[1:]:
        begin = jnp.where(row_at >= start, start, begin)
    allowed = (key_pos >= begin) & (key_pos <= row_pos)
    return slice(q0, w1), slice(w0, w1), jnp.where(allowed, 0.0, -1e30).astype(f32)


def stacked(whole, rows, heads):
    return jnp.concatenate([whole[rows, h * HEAD_DIM : (h + 1) * HEAD_DIM] for h in range(heads)], axis=0)


def side_by_side(value, heads):
    return jnp.concatenate([value[h * Q_BLOCK : (h + 1) * Q_BLOCK, :] for h in range(heads)], axis=1)


def forward_kernel(groups, me_ref, lengths_ref, *refs):
    pieces, outs = refs[:groups], refs[groups + 1 : 2 * groups + 1]
    o_ref, stats_ref, q_all, kv_all, attn_all = refs[2 * groups + 1 :]
    u = me_ref[0]
    length, qw = q_all.shape
    heads = qw // HEAD_DIM
    collect(u, pieces, (q_all, SCALE), (kv_all, None))
    starts = doc_starts(lengths_ref)
    for b in range(length // Q_BLOCK):
        here, there, bias = window(b, starts)
        keys, values = kv_all[there, :HEAD_DIM], kv_all[there, HEAD_DIM:]
        scores = nt(stacked(q_all, here, heads), keys)
        scores = scores + jnp.concatenate([bias] * heads, axis=0)
        peak = jnp.max(scores, axis=1, keepdims=True)
        weights = jnp.exp(scores - peak)
        inverse = 1.0 / jnp.sum(weights, axis=1, keepdims=True)
        mixed = side_by_side(nn((weights * inverse).astype(bf16), values), heads)
        o_ref[here, :] = mixed
        attn_all[here, :] = mixed.astype(bf16)
        stats_ref[b, :, :1] = peak
        stats_ref[b, :, 1:2] = inverse
    rows = length // groups
    for g in range(groups):
        hand_out(u, g, attn_all[g * rows : (g + 1) * rows, :], outs)


def backward_kernel(groups, me_ref, lengths_ref, cos_ref, sin_ref, o_ref, stats_ref, *refs):
    qkv_pieces, g_all = refs[:groups], refs[groups]
    q_all, kv_all, dq_all, acc = refs[-4:]
    outs = refs[-4 - groups : -4]
    u = me_ref[0]
    length, qw = q_all.shape
    heads = qw // HEAD_DIM
    collect(u, qkv_pieces, (q_all, SCALE), (kv_all, None))
    starts = doc_starts(lengths_ref)
    acc[...] = jnp.zeros_like(acc)
    for b in range(length // Q_BLOCK):
        here, there, bias = window(b, starts)
        keys, values = kv_all[there, :HEAD_DIM], kv_all[there, HEAD_DIM:]
        queries, grads = stacked(q_all, here, heads), stacked(g_all, here, heads)
        scores = nt(queries, keys) + jnp.concatenate([bias] * heads, axis=0)
        shares = jnp.exp(scores - stats_ref[b, :, :1]) * stats_ref[b, :, 1:2]
        row_dot = jnp.sum(grads.astype(f32) * stacked(o_ref, here, heads), axis=1, keepdims=True)
        d_scores = (shares * (nt(grads, values) - row_dot)).astype(bf16)
        dq_all[here, :] = side_by_side(nn(d_scores, keys) * SCALE, heads)
        acc[:HEAD_DIM, there] += tn(queries, d_scores)
        acc[HEAD_DIM:, there] += tn(grads, shares.astype(bf16))
    rows = length // groups
    lower = lower_lanes(rows)
    value_lane = lax.broadcasted_iota(jnp.int32, (rows, 128), 1) >= HEAD_DIM
    for g in range(groups):
        here = slice(g * rows, (g + 1) * rows)
        cos, sin = cos_ref[here, :], sin_ref[here, :]
        parts = []
        for c in range(qw // 128):
            x = dq_all[here, c * 128 : (c + 1) * 128]
            parts.append(x * cos - turn(x, lower) * sin)
        x = acc[:, here].T
        parts.append(jnp.where(value_lane, x, x * cos - turn(x, lower) * sin))
        hand_out(u, g, jnp.concatenate(parts, axis=1).astype(bf16), outs)


def join_attn_kernel(groups, me_ref, *refs):
    u, out = me_ref[0], refs[-1]
    qw = QW // groups
    for j in range(groups):
        at = pl.multiple_of((u ^ j) * qw, qw)
        out[:, pl.ds(at, qw)] = refs[j][...]


def join_proj_kernel(groups, me_ref, *refs):
    u, (out, wide) = me_ref[0], refs[-2:]
    qw = QW // groups
    repeat = groups // KV_HEADS
    wide[...] = jnp.zeros_like(wide)
    for j in range(groups):
        at = pl.multiple_of((u ^ j) * qw, qw)
        out[:, pl.ds(at, qw)] = refs[j][:, :qw]
        back = refs[j][:, qw:].astype(f32)
        for kh in range(KV_HEADS):

            @pl.when((u ^ j) // repeat == kh)
            def _():
                wide[:, kh * 128 : (kh + 1) * 128] += back

    low = wide[...].astype(bf16)
    for at, half in ((QW, 0), (QW + KW, HEAD_DIM)):
        heads = [low[:, kh * 128 + half : kh * 128 + half + HEAD_DIM] for kh in range(KV_HEADS)]
        out[:, at : at + KW] = jnp.concatenate(heads, axis=1)


def tokens_kernel(slots, many, groups, factor, me_ref, tok_ref, d_out_ref, d_proj_ref, *refs):
    n = len(slots)
    d_tok_ref, d_gain_ref, wide, gains = refs[-4:]
    d = me_ref[1]
    width = tok_ref.shape[1]
    part = width // n
    d_proj = d_proj_ref[...]
    for j in range(n):
        at = pl.multiple_of((d ^ j) * part, part)
        w, ext = whole_slot(refs, slots[j], part)
        wide[:, pl.ds(at, part)] = nt(d_proj, w[:, : d_proj.shape[1]])
        gains[:, pl.ds(at, part)] = ext[part : part + 1, :part].astype(f32)
    x = tok_ref[...].astype(f32)
    inv = inverse_rms(x)
    unit = x * inv
    d_normed = wide[...]
    d_gain = jnp.sum(d_normed * unit, axis=0, keepdims=True) * factor
    scaled = d_normed * gains[...]
    mean = jnp.mean(scaled * unit, axis=1, keepdims=True)
    d_tok_ref[...] = (d_out_ref[...].astype(f32) + inv * (scaled - unit * mean)).astype(bf16)
    block = width // (groups * n)
    for e in range(n):
        starts = [g * (width // groups) + e * block for g in range(groups)]
        mine = jnp.concatenate([d_gain[:, s : s + block] for s in starts], axis=1)
        for g in range(groups):
            d_gain_ref[g, e : e + 1, :] = mine[:, g * block : (g + 1) * block]


def grads_kernel(slots, side, groups, factor, me_ref, slices, *refs):
    n = len(slots)
    out, acc = refs[-2:]
    d = me_ref[1]
    kept = acc.shape[0]
    for j in range(n):
        a = slices[d ^ j, side * kept : (side + 1) * kept, :]
        b, _ = whole_slot(refs, slots[j], a.shape[1])
        term = nn(a, b)
        if j == 0:
            acc[...] = term
        else:
            acc[...] += term
    block = kept // groups
    for g in range(groups):
        out[g] = acc[g * block : (g + 1) * block, :] * factor


def grads_and_pass_kernel(slots, side, groups, factor, me_ref, slices, *refs):
    *refs, pass_ref, out, pass_out, acc = refs
    grads_kernel(slots, side, groups, factor, me_ref, slices, *refs, out, acc)
    pass_out[...] = pass_ref[...]


def block_sum(local, axis):
    me = lax.axis_index(axis)
    total = lax.dynamic_index_in_dim(local, me, 0, keepdims=False)
    for j in range(1, lax.axis_size(axis)):
        total = total + swap(lax.dynamic_index_in_dim(local, me ^ j, 0, keepdims=False), axis, j)
    return total


def weights_here(w_qkv, w_out, gain, me, qw, grad_rows):
    part, columns = w_qkv.shape
    rows, width = grad_rows.shape
    half = rows // 2

    def kernel(me_ref, w_qkv_ref, w_out_ref, gain_ref, grad_ref, out, upper, lower):
        at = pl.multiple_of(me_ref[0] * qw, qw)
        out[:part, :columns] = w_qkv_ref[...]
        out[:part, columns:] = w_out_ref[:, pl.ds(at, qw)]
        out[part:, :] = jnp.zeros_like(out[part:, :])
        out[part : part + 1, :part] = gain_ref[...]
        upper[...] = grad_ref[:half, :]
        lower[...] = grad_ref[half:, :]

    return pl.pallas_call(
        kernel,
        out_shape=[shape(part + 16, columns + qw)] + [shape(half, width)] * 2,
        in_specs=[SMEM] + [VMEM] * 4,
        out_specs=[VMEM] * 3,
        cost_estimate=about(2),
        name="weights_here",
    )(me, w_qkv, w_out, gain[None, :], grad_rows)


def shape(*dims, dtype=bf16):
    return jax.ShapeDtypeStruct(dims, dtype)


def body(tokens, d_out, lengths, gain, w_qkv, w_out):
    groups, n = lax.axis_size("ulysses"), lax.axis_size("dp")
    u, d = lax.axis_index("ulysses"), lax.axis_index("dp")
    me = jnp.stack([u, d]).astype(jnp.int32)
    token_rows, grad_rows = tokens[0], d_out[0]
    rows, width = token_rows.shape
    length = rows * groups
    part = width // n
    heads = HEADS // groups
    qw = heads * HEAD_DIM
    columns = w_qkv.shape[1]
    factor = 1.0 / math.sqrt(length * n)
    block = width // (groups * n)
    kept = block * groups

    held, *grad_halves = weights_here(w_qkv, w_out, gain, me, qw, grad_rows)
    held_near = neighbours(held, "dp")
    first, second = (spread(half, "ulysses") for half in grad_halves)
    held_arrays, held_slots = complete(*relay(held, *held_near, first[1], first[groups - 1]), "dp")

    bounds = jnp.cumsum(lengths[0]) - lengths[0]
    places = jnp.arange(length, dtype=jnp.int32)
    begins = jnp.max(jnp.where(bounds[None, :] <= places[:, None], bounds[None, :], 0), axis=1)
    places = places - begins
    inverse = ROPE_BASE ** (-jnp.arange(0, HEAD_DIM, 2).astype(f32) / HEAD_DIM)
    angles = places.astype(f32)[:, None] * jnp.tile(inverse, 4)[None, :]
    signs = jnp.where(jnp.arange(128) % HEAD_DIM < HEAD_DIM // 2, -1.0, 1.0).astype(f32)
    cos, sin = jnp.cos(angles), jnp.sin(angles) * signs[None, :]
    cos_here = lax.dynamic_slice_in_dim(cos, u * rows, rows)
    sin_here = lax.dynamic_slice_in_dim(sin, u * rows, rows)

    *pieces, normed = pl.pallas_call(
        functools.partial(proj_kernel, held_slots, len(held_arrays), groups),
        out_shape=[shape(rows, qw + 128)] * groups + [shape(rows, width)],
        in_specs=[SMEM] + [VMEM] * (3 + len(held_arrays)) + [ANY] * 2,
        out_specs=[VMEM] * (groups + 1),
        scratch_shapes=[pltpu.VMEM((rows, columns), f32)],
        compiler_params=params(56),
        cost_estimate=about(8),
        name="proj",
    )(me, token_rows, cos_here, sin_here, *held_arrays, second[1], second[groups - 1])
    qkv_here = [pieces[0]] + [swap(pieces[j], "ulysses", j) for j in range(1, groups)]

    own_slices = pl.pallas_call(
        functools.partial(slices_kernel, n, groups),
        out_shape=shape(n, 2 * kept, rows),
        in_specs=[VMEM] * 2,
        out_specs=VMEM,
        scratch_shapes=[pltpu.VMEM((width, rows), bf16)],
        compiler_params=params(56),
        cost_estimate=about(3),
        name="slices",
    )(normed, grad_rows)
    slices = lax.all_to_all(own_slices, "dp", 0, 0, tiled=True)
    d_attn = pl.pallas_call(
        functools.partial(d_attn_kernel, held_slots, groups, columns),
        out_shape=shape(length, qw),
        in_specs=[SMEM] + [VMEM] * (2 * groups + len(held_arrays)) + [ANY],
        out_specs=VMEM,
        scratch_shapes=[pltpu.VMEM((width, qw), bf16)],
        compiler_params=params(56),
        cost_estimate=about(6),
        name="d_attn",
    )(me, *first, *second, *held_arrays, own_slices)

    blocks = length // Q_BLOCK
    *mixed, o, stats = pl.pallas_call(
        functools.partial(forward_kernel, groups),
        out_shape=[shape(rows, qw)] * groups
        + [shape(length, qw, dtype=f32), shape(blocks, heads * Q_BLOCK, 2, dtype=f32)],
        in_specs=[SMEM] * 2 + [VMEM] * groups + [ANY],
        out_specs=[VMEM] * (groups + 2),
        scratch_shapes=[
            pltpu.VMEM((length, qw), bf16),
            pltpu.VMEM((length, 128), bf16),
            pltpu.VMEM((length, qw), bf16),
        ],
        compiler_params=params(56),
        cost_estimate=about(10),
        name="forward",
    )(me, lengths[0], *qkv_here, d_attn)
    mixed = [mixed[0]] + [swap(mixed[j], "ulysses", j) for j in range(1, groups)]

    back = pl.pallas_call(
        functools.partial(backward_kernel, groups),
        out_shape=[shape(rows, qw + 128)] * groups,
        in_specs=[SMEM] * 2 + [VMEM] * (5 + groups),
        out_specs=[VMEM] * groups,
        scratch_shapes=[
            pltpu.VMEM((length, qw), bf16),
            pltpu.VMEM((length, 128), bf16),
            pltpu.VMEM((length, qw), f32),
            pltpu.VMEM((128, length), f32),
        ],
        compiler_params=params(56),
        cost_estimate=about(15),
        name="backward",
    )(me, lengths[0], cos, sin, o, stats, *qkv_here, d_attn)
    back = [back[0]] + [swap(back[j], "ulysses", j) for j in range(1, groups)]

    attn = pl.pallas_call(
        functools.partial(join_attn_kernel, groups),
        out_shape=shape(rows, QW),
        in_specs=[SMEM] + [VMEM] * groups + [ANY] * 2,
        out_specs=VMEM,
        cost_estimate=about(2),
        name="join_attn",
    )(me, *mixed, slices, back[0])
    attn_near = neighbours(attn, "dp")

    d_proj = pl.pallas_call(
        functools.partial(join_proj_kernel, groups),
        out_shape=shape(rows, columns),
        in_specs=[SMEM] + [VMEM] * groups + [ANY] * 2,
        out_specs=VMEM,
        scratch_shapes=[pltpu.VMEM((rows, 128 * KV_HEADS), f32)],
        cost_estimate=about(3),
        name="join_proj",
    )(me, *back, *attn_near)
    proj_near = neighbours(d_proj, "dp")
    attn_arrays, attn_slots = complete(*relay(attn, *attn_near, d_proj), "dp")

    d_w_out_terms = pl.pallas_call(
        functools.partial(grads_kernel, attn_slots, 1, groups, factor),
        out_shape=shape(groups, block, QW, dtype=f32),
        in_specs=[SMEM] + [VMEM] * (1 + len(attn_arrays)),
        out_specs=VMEM,
        scratch_shapes=[pltpu.VMEM((kept, QW), f32)],
        compiler_params=params(56),
        cost_estimate=about(5),
        name="d_w_out",
    )(me, slices, *attn_arrays)

    d_w_out = block_sum(d_w_out_terms, "ulysses")
    relayed = relay(d_proj, *proj_near, d_w_out_terms)
    proj_arrays, proj_slots = complete(*relayed, "dp")

    d_tokens, partial_gain = pl.pallas_call(
        functools.partial(tokens_kernel, held_slots, len(held_arrays), groups, factor),
        out_shape=[shape(rows, width), shape(groups, n, block, dtype=f32)],
        in_specs=[SMEM] + [VMEM] * (3 + len(held_arrays)) + [ANY],
        out_specs=[VMEM] * 2,
        scratch_shapes=[pltpu.VMEM((rows, width), f32), pltpu.VMEM((1, width), f32)],
        compiler_params=params(56),
        cost_estimate=about(8),
        name="d_tokens",
    )(me, token_rows, grad_rows, d_proj, *held_arrays, relayed[0])

    d_w_qkv, gain_terms = pl.pallas_call(
        functools.partial(grads_and_pass_kernel, proj_slots, 0, groups, factor),
        out_shape=[shape(groups, block, columns, dtype=f32), shape(groups, n, block, dtype=f32)],
        in_specs=[SMEM] + [VMEM] * (2 + len(proj_arrays)),
        out_specs=[VMEM] * 2,
        scratch_shapes=[pltpu.VMEM((kept, columns), f32)],
        compiler_params=params(56),
        cost_estimate=about(6),
        name="d_w_qkv",
    )(me, slices, *proj_arrays, partial_gain)
    d_w_qkv = block_sum(d_w_qkv, "ulysses")
    d_gain = gain_terms.reshape(groups * n, block)
    d_gain = lax.all_to_all(d_gain, ("ulysses", "dp"), 0, 0, tiled=True).sum(axis=0)
    return (d_tokens[None], d_w_qkv, d_w_out, d_gain)


def solution(mesh):
    in_specs = (
        P("dp", "ulysses", None),
        P("dp", "ulysses", None),
        P("dp", None),
        P("dp"),
        P("dp", None),
        P("dp", None),
    )
    out_specs = (
        P("dp", "ulysses", None),
        P(("ulysses", "dp"), None),
        P(("ulysses", "dp"), None),
        P(("ulysses", "dp")),
    )
    return jax.shard_map(body, mesh=mesh, in_specs=in_specs, out_specs=out_specs, check_vma=False)
```

```python
import functools
import math

import jax
import jax.numpy as jnp
from jax import lax
from jax.experimental import pallas as pl
from jax.experimental.pallas import tpu as pltpu
from jax.sharding import PartitionSpec as P

HEADS = 16
KV_HEADS = 4
HEAD_DIM = 64
QW = 1024
KW = 256
DOC_MOST = 384
Q_BLOCK = 128

EPS = 1e-05
ROPE_BASE = 500000.0
SCALE = HEAD_DIM ** (-0.5)

bf16 = jnp.bfloat16
f32 = jnp.float32


def params(mib):
    return pltpu.CompilerParams(vmem_limit_bytes=mib << 20)


def about(us):
    return pl.CostEstimate(flops=int(us * 1e9), bytes_accessed=int(us * 3e6), transcendentals=0)


SMEM = pl.BlockSpec(memory_space=pltpu.SMEM)
VMEM = pl.BlockSpec(memory_space=pltpu.VMEM)
ANY = pl.BlockSpec(memory_space=pl.ANY)


def nt(a, b):
    return lax.dot_general(a, b, (((1,), (1,)), ((), ())), preferred_element_type=f32)


def tn(a, b):
    return lax.dot_general(a, b, (((0,), (0,)), ((), ())), preferred_element_type=f32)


def nn(a, b):
    return jnp.dot(a, b, preferred_element_type=f32)


def swap(a, axis, bit):
    n = lax.axis_size(axis)
    return lax.ppermute(a, axis, [(i, i ^ bit) for i in range(n)])


def neighbours(a, axis):
    n = lax.axis_size(axis)
    return swap(a, axis, n // 4), swap(a, axis, n // 2)


def complete(own, first, second, axis):
    n = lax.axis_size(axis)
    rows = own.shape[0]
    half = rows // 32 * 16
    arrays = [own, first, second, swap(first[:half], axis, n // 2), swap(second[half:], axis, n // 4)]
    slots = {
        0: [(0, 0, rows)],
        n // 4: [(1, 0, rows)],
        n // 2: [(2, 0, rows)],
        n // 4 | n // 2: [(3, 0, half), (4, 0, rows - half)],
    }
    bit = n // 8
    while bit >= 1:
        at = len(arrays)
        arrays += [swap(a, axis, bit) for a in arrays]
        for j in list(slots):
            slots[j ^ bit] = [(i + at, start, size) for i, start, size in slots[j]]
        bit //= 2
    return arrays, [slots[j] for j in range(n)]


def whole_slot(refs, pieces, rows):
    values = [refs[i][start : start + size, :] for i, start, size in pieces]
    value = values[0] if len(values) == 1 else jnp.concatenate(values, axis=0)
    return value[:rows], value


def turn(x, lower):
    return jnp.where(lower, pltpu.roll(x, 96, 1), pltpu.roll(x, 32, 1))


def lower_lanes(rows):
    return lax.broadcasted_iota(jnp.int32, (rows, 128), 1) % HEAD_DIM < HEAD_DIM // 2


def inverse_rms(x):
    return lax.rsqrt(jnp.mean(x * x, axis=1, keepdims=True) + EPS)


def proj_kernel(slots, many, groups, me_ref, tok_ref, cos_ref, sin_ref, *refs):
    n = len(slots)
    outs, (normed_ref, acc) = refs[-groups - 2 : -2], refs[-2:]
    u, d = me_ref[0], me_ref[1]
    rows, width = tok_ref.shape
    part = width // n
    inv = inverse_rms(tok_ref[...].astype(f32))
    for j in range(n):
        at = pl.multiple_of((d ^ j) * part, part)
        w, ext = whole_slot(refs, slots[j], part)
        gain = ext[part : part + 1, :part].astype(f32)
        normed = (tok_ref[:, pl.ds(at, part)].astype(f32) * inv * gain).astype(bf16)
        normed_ref[:, pl.ds(at, part)] = normed
        term = nn(normed, w[:, : acc.shape[1]])
        if j == 0:
            acc[...] = term
        else:
            acc[...] += term
    lower = lower_lanes(rows)
    cos, sin = cos_ref[...], sin_ref[...]
    turned = []
    for c in range((QW + KW) // 128):
        x = acc[:, c * 128 : (c + 1) * 128]
        turned.append((x * cos + turn(x, lower) * sin).astype(bf16))
    heads = HEADS // groups
    repeat = groups // KV_HEADS
    for g in range(groups):
        qw = heads * HEAD_DIM
        q = jnp.concatenate(turned[g * qw // 128 : (g + 1) * qw // 128], axis=1)
        kh = g // repeat
        at = QW // 128 + kh // 2
        half = (kh % 2) * HEAD_DIM
        k = turned[at][:, half : half + HEAD_DIM]
        v = acc[:, QW + KW + kh * HEAD_DIM : QW + KW + (kh + 1) * HEAD_DIM].astype(bf16)
        piece = jnp.concatenate([q, k, v], axis=1)
        for j in range(groups):

            @pl.when((u ^ g) == j)
            def _():
                outs[j][...] = piece


def d_attn_kernel(slots, sets, columns, me_ref, own_ref, pair_ref, *refs):
    outs, weight = refs[-1 - sets : -1], refs[-1]
    u, d = me_ref[0], me_ref[1]
    n = len(slots)
    rows, width = own_ref.shape
    part = width // n
    for j in range(n):
        at = pl.multiple_of((d ^ j) * part, part)
        weight[pl.ds(at, part), :] = whole_slot(refs, slots[j], part)[0][:, columns:]
    for side, ref in enumerate((own_ref, pair_ref)):
        at = pl.ds(pl.multiple_of((u % 2 ^ side) * rows, rows), rows)
        value = nn(ref[...], weight[...]).astype(bf16)
        qw = value.shape[1] // sets
        for i in range(sets):
            outs[i][at, :] = value[:, i * qw : (i + 1) * qw]


def slices_kernel(n, groups, normed_ref, d_out_ref, *refs):
    out, turned = refs[-2:]
    width = normed_ref.shape[1]
    block = width // (groups * n)
    for side, ref in enumerate((normed_ref, d_out_ref)):
        turned[...] = ref[...].T
        for e in range(n):
            for g in range(groups):
                at = g * (width // groups) + e * block
                to = (side * groups + g) * block
                out[e, to : to + block, :] = turned[at : at + block, :]


def collect(u, pieces, *wholes):
    rows = pieces[0].shape[0]
    for j, piece in enumerate(pieces):
        at = pl.ds(pl.multiple_of((u ^ j) * rows, rows), rows)
        lane = 0
        for whole, scale in wholes:
            part = piece[:, lane : lane + whole.shape[1]]
            whole[at, :] = part if scale is None else part * jnp.asarray(scale, bf16)
            lane += whole.shape[1]


def hand_out(u, g, value, outs):
    for j, out in enumerate(outs):

        @pl.when((u ^ g) == j)
        def _():
            out[...] = value.astype(out.dtype)


def doc_starts(lengths_ref):
    starts = [jnp.int32(0)]
    for i in range(lengths_ref.shape[0] - 1):
        starts.append(starts[-1] + lengths_ref[i])
    return starts


def window(b, starts):
    q0 = b * Q_BLOCK
    w0, w1 = max(0, q0 - DOC_MOST), q0 + Q_BLOCK
    key_pos = w0 + lax.broadcasted_iota(jnp.int32, (Q_BLOCK, w1 - w0), 1)
    row_pos = q0 + lax.broadcasted_iota(jnp.int32, (Q_BLOCK, w1 - w0), 0)
    row_at = q0 + lax.broadcasted_iota(jnp.int32, (Q_BLOCK, 1), 0)
    begin = jnp.zeros((Q_BLOCK, 1), jnp.int32)
    for start in starts[1:]:
        begin = jnp.where(row_at >= start, start, begin)
    allowed = (key_pos >= begin) & (key_pos <= row_pos)
    return slice(q0, w1), slice(w0, w1), jnp.where(allowed, 0.0, -1e30).astype(f32)


def stacked(whole, rows, heads):
    return jnp.concatenate([whole[rows, h * HEAD_DIM : (h + 1) * HEAD_DIM] for h in range(heads)], axis=0)


def side_by_side(value, heads):
    return jnp.concatenate([value[h * Q_BLOCK : (h + 1) * Q_BLOCK, :] for h in range(heads)], axis=1)


def forward_kernel(groups, me_ref, lengths_ref, *refs):
    pieces, outs = refs[:groups], refs[groups + 1 : 2 * groups + 1]
    o_ref, stats_ref, q_all, kv_all, attn_all = refs[2 * groups + 1 :]
    u = me_ref[0]
    length, qw = q_all.shape
    heads = qw // HEAD_DIM
    collect(u, pieces, (q_all, SCALE), (kv_all, None))
    starts = doc_starts(lengths_ref)
    for b in range(length // Q_BLOCK):
        here, there, bias = window(b, starts)
        keys, values = kv_all[there, :HEAD_DIM], kv_all[there, HEAD_DIM:]
        scores = nt(stacked(q_all, here, heads), keys)
        scores = scores + jnp.concatenate([bias] * heads, axis=0)
        peak = jnp.max(scores, axis=1, keepdims=True)
        weights = jnp.exp(scores - peak)
        inverse = 1.0 / jnp.sum(weights, axis=1, keepdims=True)
        mixed = side_by_side(nn((weights * inverse).astype(bf16), values), heads)
        o_ref[here, :] = mixed
        attn_all[here, :] = mixed.astype(bf16)
        stats_ref[b, :, :1] = peak
        stats_ref[b, :, 1:2] = inverse
    rows = length // groups
    for g in range(groups):
        hand_out(u, g, attn_all[g * rows : (g + 1) * rows, :], outs)


def backward_kernel(groups, me_ref, lengths_ref, cos_ref, sin_ref, o_ref, stats_ref, *refs):
    qkv_pieces, grad_pieces = refs[:groups], refs[groups : groups + groups // 2]
    q_all, kv_all, g_all, dq_all, acc = refs[-5:]
    outs = refs[-5 - groups : -5]
    u = me_ref[0]
    length, qw = q_all.shape
    heads = qw // HEAD_DIM
    collect(u, qkv_pieces, (q_all, SCALE), (kv_all, None))
    collect(u // 2, grad_pieces, (g_all, None))
    starts = doc_starts(lengths_ref)
    acc[...] = jnp.zeros_like(acc)
    for b in range(length // Q_BLOCK):
        here, there, bias = window(b, starts)
        keys, values = kv_all[there, :HEAD_DIM], kv_all[there, HEAD_DIM:]
        queries, grads = stacked(q_all, here, heads), stacked(g_all, here, heads)
        scores = nt(queries, keys) + jnp.concatenate([bias] * heads, axis=0)
        shares = jnp.exp(scores - stats_ref[b, :, :1]) * stats_ref[b, :, 1:2]
        row_dot = jnp.sum(grads.astype(f32) * stacked(o_ref, here, heads), axis=1, keepdims=True)
        d_scores = (shares * (nt(grads, values) - row_dot)).astype(bf16)
        dq_all[here, :] = side_by_side(nn(d_scores, keys) * SCALE, heads)
        acc[:HEAD_DIM, there] += tn(queries, d_scores)
        acc[HEAD_DIM:, there] += tn(grads, shares.astype(bf16))
    rows = length // groups
    lower = lower_lanes(rows)
    value_lane = lax.broadcasted_iota(jnp.int32, (rows, 128), 1) >= HEAD_DIM
    for g in range(groups):
        here = slice(g * rows, (g + 1) * rows)
        cos, sin = cos_ref[here, :], sin_ref[here, :]
        parts = []
        for c in range(qw // 128):
            x = dq_all[here, c * 128 : (c + 1) * 128]
            parts.append(x * cos - turn(x, lower) * sin)
        x = acc[:, here].T
        parts.append(jnp.where(value_lane, x, x * cos - turn(x, lower) * sin))
        hand_out(u, g, jnp.concatenate(parts, axis=1).astype(bf16), outs)


def join_attn_kernel(groups, me_ref, *refs):
    u, out = me_ref[0], refs[-1]
    qw = QW // groups
    for j in range(groups):
        at = pl.multiple_of((u ^ j) * qw, qw)
        out[:, pl.ds(at, qw)] = refs[j][...]


def join_proj_kernel(groups, me_ref, *refs):
    u, (out, wide) = me_ref[0], refs[-2:]
    qw = QW // groups
    repeat = groups // KV_HEADS
    wide[...] = jnp.zeros_like(wide)
    for j in range(groups):
        at = pl.multiple_of((u ^ j) * qw, qw)
        out[:, pl.ds(at, qw)] = refs[j][:, :qw]
        back = refs[j][:, qw:].astype(f32)
        for kh in range(KV_HEADS):

            @pl.when((u ^ j) // repeat == kh)
            def _():
                wide[:, kh * 128 : (kh + 1) * 128] += back

    low = wide[...].astype(bf16)
    for at, half in ((QW, 0), (QW + KW, HEAD_DIM)):
        heads = [low[:, kh * 128 + half : kh * 128 + half + HEAD_DIM] for kh in range(KV_HEADS)]
        out[:, at : at + KW] = jnp.concatenate(heads, axis=1)


def tokens_kernel(slots, many, groups, factor, me_ref, tok_ref, d_out_ref, d_proj_ref, *refs):
    n = len(slots)
    d_tok_ref, d_gain_ref, wide, gains = refs[-4:]
    d = me_ref[1]
    width = tok_ref.shape[1]
    part = width // n
    d_proj = d_proj_ref[...]
    for j in range(n):
        at = pl.multiple_of((d ^ j) * part, part)
        w, ext = whole_slot(refs, slots[j], part)
        wide[:, pl.ds(at, part)] = nt(d_proj, w[:, : d_proj.shape[1]])
        gains[:, pl.ds(at, part)] = ext[part : part + 1, :part].astype(f32)
    x = tok_ref[...].astype(f32)
    inv = inverse_rms(x)
    unit = x * inv
    d_normed = wide[...]
    d_gain = jnp.sum(d_normed * unit, axis=0, keepdims=True) * factor
    scaled = d_normed * gains[...]
    mean = jnp.mean(scaled * unit, axis=1, keepdims=True)
    d_tok_ref[...] = (d_out_ref[...].astype(f32) + inv * (scaled - unit * mean)).astype(bf16)
    block = width // (groups * n)
    for e in range(n):
        starts = [g * (width // groups) + e * block for g in range(groups)]
        mine = jnp.concatenate([d_gain[:, s : s + block] for s in starts], axis=1)
        for g in range(groups):
            d_gain_ref[g, e : e + 1, :] = mine[:, g * block : (g + 1) * block]


def grads_kernel(slots, side, groups, factor, me_ref, slices, *refs):
    n = len(slots)
    outs, acc = refs[-1 - groups : -1], refs[-1]
    u, d = me_ref[0], me_ref[1]
    kept = acc.shape[0]
    for j in range(n):
        a = slices[d ^ j, side * kept : (side + 1) * kept, :]
        b, _ = whole_slot(refs, slots[j], a.shape[1])
        term = nn(a, b)
        if j == 0:
            acc[...] = term
        else:
            acc[...] += term
    block = kept // groups
    for g in range(groups):
        hand_out(u, g, acc[g * block : (g + 1) * block, :] * factor, outs)


def grads_and_pass_kernel(slots, side, groups, factor, me_ref, slices, *refs):
    refs, (pass_ref, *outs, pass_out, acc) = refs[: -3 - groups], refs[-3 - groups :]
    grads_kernel(slots, side, groups, factor, me_ref, slices, *refs, *outs, acc)
    pass_out[...] = pass_ref[...]


def weights_here(w_qkv, w_out, gain, me, qw):
    part, columns = w_qkv.shape
    sets = QW // qw // 2

    def kernel(me_ref, w_qkv_ref, w_out_ref, gain_ref, out):
        out[:part, :columns] = w_qkv_ref[...]
        for i in range(sets):
            at = pl.multiple_of((me_ref[0] ^ (2 * i)) * qw, qw)
            out[:part, columns + i * qw : columns + (i + 1) * qw] = w_out_ref[:, pl.ds(at, qw)]
        out[part:, :] = jnp.zeros_like(out[part:, :])
        out[part : part + 1, :part] = gain_ref[...]

    return pl.pallas_call(
        kernel,
        out_shape=shape(part + 16, columns + sets * qw),
        in_specs=[SMEM] + [VMEM] * 3,
        out_specs=VMEM,
        cost_estimate=about(2),
        name="weights_here",
    )(me, w_qkv, w_out, gain[None, :])


def after(value, *earlier):
    def kernel(*refs):
        del refs

    return pl.pallas_call(
        kernel,
        out_shape=shape(*value.shape),
        in_specs=[ANY] * (1 + len(earlier)),
        out_specs=ANY,
        input_output_aliases={0: 0},
        cost_estimate=about(0.1),
        name="after",
    )(value, *earlier)


def shape(*dims, dtype=bf16):
    return jax.ShapeDtypeStruct(dims, dtype)


def body(tokens, d_out, lengths, gain, w_qkv, w_out):
    groups, n = lax.axis_size("ulysses"), lax.axis_size("dp")
    u, d = lax.axis_index("ulysses"), lax.axis_index("dp")
    me = jnp.stack([u, d]).astype(jnp.int32)
    token_rows, grad_rows = tokens[0], d_out[0]
    rows, width = token_rows.shape
    length = rows * groups
    part = width // n
    heads = HEADS // groups
    qw = heads * HEAD_DIM
    columns = w_qkv.shape[1]
    factor = 1.0 / math.sqrt(length * n)
    block = width // (groups * n)
    kept = block * groups

    held = weights_here(w_qkv, w_out, gain, me, qw)
    held_near = neighbours(held, "dp")
    grad_pair = swap(grad_rows, "ulysses", 1)
    held_arrays, held_slots = complete(held, after(held_near[0], grad_pair), held_near[1], "dp")

    bounds = jnp.cumsum(lengths[0]) - lengths[0]
    places = jnp.arange(length, dtype=jnp.int32)
    begins = jnp.max(jnp.where(bounds[None, :] <= places[:, None], bounds[None, :], 0), axis=1)
    places = places - begins
    inverse = ROPE_BASE ** (-jnp.arange(0, HEAD_DIM, 2).astype(f32) / HEAD_DIM)
    angles = places.astype(f32)[:, None] * jnp.tile(inverse, 4)[None, :]
    signs = jnp.where(jnp.arange(128) % HEAD_DIM < HEAD_DIM // 2, -1.0, 1.0).astype(f32)
    cos, sin = jnp.cos(angles), jnp.sin(angles) * signs[None, :]
    cos_here = lax.dynamic_slice_in_dim(cos, u * rows, rows)
    sin_here = lax.dynamic_slice_in_dim(sin, u * rows, rows)

    *pieces, normed = pl.pallas_call(
        functools.partial(proj_kernel, held_slots, len(held_arrays), groups),
        out_shape=[shape(rows, qw + 128)] * groups + [shape(rows, width)],
        in_specs=[SMEM] + [VMEM] * (3 + len(held_arrays)),
        out_specs=[VMEM] * (groups + 1),
        scratch_shapes=[pltpu.VMEM((rows, columns), f32)],
        compiler_params=params(56),
        cost_estimate=about(8),
        name="proj",
    )(me, token_rows, cos_here, sin_here, *held_arrays)
    qkv_here = [pieces[0]] + [swap(pieces[j], "ulysses", j) for j in range(1, groups)]

    own_slices = pl.pallas_call(
        functools.partial(slices_kernel, n, groups),
        out_shape=shape(n, 2 * kept, rows),
        in_specs=[VMEM] * 2,
        out_specs=VMEM,
        scratch_shapes=[pltpu.VMEM((width, rows), bf16)],
        compiler_params=params(56),
        cost_estimate=about(3),
        name="slices",
    )(normed, grad_rows)
    slices = lax.all_to_all(own_slices, "dp", 0, 0, tiled=True)
    sets = groups // 2
    pieces = pl.pallas_call(
        functools.partial(d_attn_kernel, held_slots, sets, columns),
        out_shape=[shape(2 * rows, qw)] * sets,
        in_specs=[SMEM] + [VMEM] * (2 + len(held_arrays)) + [ANY],
        out_specs=[VMEM] * sets,
        scratch_shapes=[pltpu.VMEM((width, sets * qw), bf16)],
        compiler_params=params(56),
        cost_estimate=about(6),
        name="d_attn",
    )(me, grad_rows, grad_pair, *held_arrays, qkv_here[1])
    grads_here = [pieces[0]] + [swap(after(pieces[i], *qkv_here[1:]), "ulysses", 2 * i) for i in range(1, sets)]

    blocks = length // Q_BLOCK
    *mixed, o, stats = pl.pallas_call(
        functools.partial(forward_kernel, groups),
        out_shape=[shape(rows, qw)] * groups
        + [shape(length, qw, dtype=f32), shape(blocks, heads * Q_BLOCK, 2, dtype=f32)],
        in_specs=[SMEM] * 2 + [VMEM] * groups + [ANY],
        out_specs=[VMEM] * (groups + 2),
        scratch_shapes=[
            pltpu.VMEM((length, qw), bf16),
            pltpu.VMEM((length, 128), bf16),
            pltpu.VMEM((length, qw), bf16),
        ],
        compiler_params=params(56),
        cost_estimate=about(10),
        name="forward",
    )(me, lengths[0], *qkv_here, own_slices)
    mixed = [mixed[0]] + [swap(mixed[j], "ulysses", j) for j in range(1, groups)]

    back = pl.pallas_call(
        functools.partial(backward_kernel, groups),
        out_shape=[shape(rows, qw + 128)] * groups,
        in_specs=[SMEM] * 2 + [VMEM] * (4 + groups + sets),
        out_specs=[VMEM] * groups,
        scratch_shapes=[
            pltpu.VMEM((length, qw), bf16),
            pltpu.VMEM((length, 128), bf16),
            pltpu.VMEM((length, qw), bf16),
            pltpu.VMEM((length, qw), f32),
            pltpu.VMEM((128, length), f32),
        ],
        compiler_params=params(56),
        cost_estimate=about(15),
        name="backward",
    )(me, lengths[0], cos, sin, o, stats, *qkv_here, *grads_here)
    back = [back[0]] + [swap(back[j], "ulysses", j) for j in range(1, groups)]

    attn = pl.pallas_call(
        functools.partial(join_attn_kernel, groups),
        out_shape=shape(rows, QW),
        in_specs=[SMEM] + [VMEM] * groups + [ANY] * 2,
        out_specs=VMEM,
        cost_estimate=about(2),
        name="join_attn",
    )(me, *mixed, slices, back[0])
    attn_near = neighbours(attn, "dp")

    d_proj = pl.pallas_call(
        functools.partial(join_proj_kernel, groups),
        out_shape=shape(rows, columns),
        in_specs=[SMEM] + [VMEM] * groups + [ANY] * 2,
        out_specs=VMEM,
        scratch_shapes=[pltpu.VMEM((rows, 128 * KV_HEADS), f32)],
        cost_estimate=about(3),
        name="join_proj",
    )(me, *back, *attn_near)
    proj_near = neighbours(d_proj, "dp")
    attn_arrays, attn_slots = complete(attn, *(after(a, d_proj) for a in attn_near), "dp")

    d_w_out, *terms = pl.pallas_call(
        functools.partial(grads_kernel, attn_slots, 1, groups, factor),
        out_shape=[shape(block, QW, dtype=f32)] * 2 + [shape(block, QW)] * (groups - 2),
        in_specs=[SMEM] + [VMEM] * (1 + len(attn_arrays)),
        out_specs=[VMEM] * groups,
        scratch_shapes=[pltpu.VMEM((kept, QW), f32)],
        compiler_params=params(56),
        cost_estimate=about(5),
        name="d_w_out",
    )(me, slices, *attn_arrays)

    out_terms = [swap(term, "ulysses", j) for j, term in enumerate(terms, 1)]

    d_tokens, partial_gain = pl.pallas_call(
        functools.partial(tokens_kernel, held_slots, len(held_arrays), groups, factor),
        out_shape=[shape(rows, width), shape(groups, n, block, dtype=f32)],
        in_specs=[SMEM] + [VMEM] * (3 + len(held_arrays)) + [ANY],
        out_specs=[VMEM] * 2,
        scratch_shapes=[pltpu.VMEM((rows, width), f32), pltpu.VMEM((1, width), f32)],
        compiler_params=params(56),
        cost_estimate=about(8),
        name="d_tokens",
    )(me, token_rows, grad_rows, d_proj, *held_arrays, d_w_out)

    proj_arrays, proj_slots = complete(d_proj, after(proj_near[0], partial_gain), after(proj_near[1], out_terms[0]), "dp")
    d_w_qkv, *terms, gain_terms = pl.pallas_call(
        functools.partial(grads_and_pass_kernel, proj_slots, 0, groups, factor),
        out_shape=[shape(block, columns, dtype=f32)] * 2 + [shape(block, columns)] * (groups - 2) + [shape(groups, n, block, dtype=f32)],
        in_specs=[SMEM] + [VMEM] * (1 + len(proj_arrays)) + [ANY] * (groups - 1) + [VMEM],
        out_specs=[VMEM] * (groups + 1),
        scratch_shapes=[pltpu.VMEM((kept, columns), f32)],
        compiler_params=params(56),
        cost_estimate=about(6),
        name="d_w_qkv",
    )(me, slices, *proj_arrays, *out_terms, partial_gain)
    for j, term in enumerate(terms, 1):
        d_w_qkv = d_w_qkv + swap(term, "ulysses", j).astype(f32)
    for term in out_terms:
        d_w_out = d_w_out + term.astype(f32)
    d_gain = gain_terms.reshape(groups * n, block)
    d_gain = lax.all_to_all(d_gain, ("ulysses", "dp"), 0, 0, tiled=True).sum(axis=0)
    return (d_tokens[None], d_w_qkv, d_w_out, d_gain)


def solution(mesh):
    in_specs = (
        P("dp", "ulysses", None),
        P("dp", "ulysses", None),
        P("dp", None),
        P("dp"),
        P("dp", None),
        P("dp", None),
    )
    out_specs = (
        P("dp", "ulysses", None),
        P(("ulysses", "dp"), None),
        P(("ulysses", "dp"), None),
        P(("ulysses", "dp")),
    )
    return jax.shard_map(body, mesh=mesh, in_specs=in_specs, out_specs=out_specs, check_vma=False)
```

```python
import functools
import math

import jax
import jax.numpy as jnp
from jax import lax
from jax.experimental import pallas as pl
from jax.experimental.pallas import tpu as pltpu
from jax.sharding import PartitionSpec as P

HEADS = 16
KV_HEADS = 4
HEAD_DIM = 64
QW = 1024
KW = 256
DOC_MOST = 384
Q_BLOCK = 128

EPS = 1e-05
ROPE_BASE = 500000.0
SCALE = HEAD_DIM ** (-0.5)

bf16 = jnp.bfloat16
f32 = jnp.float32


def params(mib):
    return pltpu.CompilerParams(vmem_limit_bytes=mib << 20)


def about(us):
    return pl.CostEstimate(flops=int(us * 1e9), bytes_accessed=int(us * 3e6), transcendentals=0)


SMEM = pl.BlockSpec(memory_space=pltpu.SMEM)
VMEM = pl.BlockSpec(memory_space=pltpu.VMEM)
ANY = pl.BlockSpec(memory_space=pl.ANY)


def nt(a, b):
    return lax.dot_general(a, b, (((1,), (1,)), ((), ())), preferred_element_type=f32)


def tn(a, b):
    return lax.dot_general(a, b, (((0,), (0,)), ((), ())), preferred_element_type=f32)


def nn(a, b):
    return jnp.dot(a, b, preferred_element_type=f32)


def swap(a, axis, bit):
    n = lax.axis_size(axis)
    return lax.ppermute(a, axis, [(i, i ^ bit) for i in range(n)])


def neighbours(a, axis):
    n = lax.axis_size(axis)
    return swap(a, axis, n // 4), swap(a, axis, n // 2)


def complete(own, first, second, axis):
    n = lax.axis_size(axis)
    rows = own.shape[0]
    half = rows // 32 * 16
    arrays = [own, first, second, swap(first[:half], axis, n // 2), swap(second[half:], axis, n // 4)]
    slots = {
        0: [(0, 0, rows)],
        n // 4: [(1, 0, rows)],
        n // 2: [(2, 0, rows)],
        n // 4 | n // 2: [(3, 0, half), (4, 0, rows - half)],
    }
    bit = n // 8
    while bit >= 1:
        at = len(arrays)
        arrays += [swap(a, axis, bit) for a in arrays]
        for j in list(slots):
            slots[j ^ bit] = [(i + at, start, size) for i, start, size in slots[j]]
        bit //= 2
    return arrays, [slots[j] for j in range(n)]


def whole_slot(refs, pieces, rows):
    values = [refs[i][start : start + size, :] for i, start, size in pieces]
    value = values[0] if len(values) == 1 else jnp.concatenate(values, axis=0)
    return value[:rows], value


def turn(x, lower):
    return jnp.where(lower, pltpu.roll(x, 96, 1), pltpu.roll(x, 32, 1))


def lower_lanes(rows):
    return lax.broadcasted_iota(jnp.int32, (rows, 128), 1) % HEAD_DIM < HEAD_DIM // 2


def inverse_rms(x):
    return lax.rsqrt(jnp.mean(x * x, axis=1, keepdims=True) + EPS)


def proj_kernel(slots, many, groups, me_ref, tok_ref, cos_ref, sin_ref, *refs):
    n = len(slots)
    outs, (normed_ref, acc) = refs[-groups - 2 : -2], refs[-2:]
    u, d = me_ref[0], me_ref[1]
    rows, width = tok_ref.shape
    part = width // n
    inv = inverse_rms(tok_ref[...].astype(f32))
    for j in range(n):
        at = pl.multiple_of((d ^ j) * part, part)
        w, ext = whole_slot(refs, slots[j], part)
        gain = ext[part : part + 1, :part].astype(f32)
        normed = (tok_ref[:, pl.ds(at, part)].astype(f32) * inv * gain).astype(bf16)
        normed_ref[:, pl.ds(at, part)] = normed
        term = nn(normed, w[:, : acc.shape[1]])
        if j == 0:
            acc[...] = term
        else:
            acc[...] += term
    lower = lower_lanes(rows)
    cos, sin = cos_ref[...], sin_ref[...]
    turned = []
    for c in range((QW + KW) // 128):
        x = acc[:, c * 128 : (c + 1) * 128]
        turned.append((x * cos + turn(x, lower) * sin).astype(bf16))
    heads = HEADS // groups
    repeat = groups // KV_HEADS
    for g in range(groups):
        qw = heads * HEAD_DIM
        q = jnp.concatenate(turned[g * qw // 128 : (g + 1) * qw // 128], axis=1)
        kh = g // repeat
        at = QW // 128 + kh // 2
        half = (kh % 2) * HEAD_DIM
        k = turned[at][:, half : half + HEAD_DIM]
        v = acc[:, QW + KW + kh * HEAD_DIM : QW + KW + (kh + 1) * HEAD_DIM].astype(bf16)
        piece = jnp.concatenate([q, k, v], axis=1)
        for j in range(groups):

            @pl.when((u ^ g) == j)
            def _():
                outs[j][...] = piece


def d_attn_kernel(slots, sets, columns, me_ref, own_ref, pair_ref, *refs):
    outs, weight = refs[-1 - sets : -1], refs[-1]
    u, d = me_ref[0], me_ref[1]
    n = len(slots)
    rows, width = own_ref.shape
    part = width // n
    for j in range(n):
        at = pl.multiple_of((d ^ j) * part, part)
        weight[pl.ds(at, part), :] = whole_slot(refs, slots[j], part)[0][:, columns:]
    for side, ref in enumerate((own_ref, pair_ref)):
        at = pl.ds(pl.multiple_of((u % 2 ^ side) * rows, rows), rows)
        value = nn(ref[...], weight[...]).astype(bf16)
        qw = value.shape[1] // sets
        for i in range(sets):
            outs[i][at, :] = value[:, i * qw : (i + 1) * qw]


def slices_kernel(n, groups, normed_ref, d_out_ref, *refs):
    out, turned = refs[-2:]
    width = normed_ref.shape[1]
    block = width // (groups * n)
    for side, ref in enumerate((normed_ref, d_out_ref)):
        turned[...] = ref[...].T
        for e in range(n):
            for g in range(groups):
                at = g * (width // groups) + e * block
                to = (side * groups + g) * block
                out[e, to : to + block, :] = turned[at : at + block, :]


def collect(u, pieces, *wholes):
    rows = pieces[0].shape[0]
    for j, piece in enumerate(pieces):
        at = pl.ds(pl.multiple_of((u ^ j) * rows, rows), rows)
        lane = 0
        for whole, scale in wholes:
            part = piece[:, lane : lane + whole.shape[1]]
            whole[at, :] = part if scale is None else part * jnp.asarray(scale, bf16)
            lane += whole.shape[1]


def hand_out(u, g, value, outs):
    for j, out in enumerate(outs):

        @pl.when((u ^ g) == j)
        def _():
            out[...] = value.astype(out.dtype)


def doc_starts(lengths_ref):
    starts = [jnp.int32(0)]
    for i in range(lengths_ref.shape[0] - 1):
        starts.append(starts[-1] + lengths_ref[i])
    return starts


def window(b, starts):
    q0 = b * Q_BLOCK
    w0, w1 = max(0, q0 - DOC_MOST), q0 + Q_BLOCK
    key_pos = w0 + lax.broadcasted_iota(jnp.int32, (Q_BLOCK, w1 - w0), 1)
    row_pos = q0 + lax.broadcasted_iota(jnp.int32, (Q_BLOCK, w1 - w0), 0)
    row_at = q0 + lax.broadcasted_iota(jnp.int32, (Q_BLOCK, 1), 0)
    begin = jnp.zeros((Q_BLOCK, 1), jnp.int32)
    for start in starts[1:]:
        begin = jnp.where(row_at >= start, start, begin)
    allowed = (key_pos >= begin) & (key_pos <= row_pos)
    return slice(q0, w1), slice(w0, w1), jnp.where(allowed, 0.0, -1e30).astype(f32)


def stacked(whole, rows, heads):
    return jnp.concatenate([whole[rows, h * HEAD_DIM : (h + 1) * HEAD_DIM] for h in range(heads)], axis=0)


def side_by_side(value, heads):
    return jnp.concatenate([value[h * Q_BLOCK : (h + 1) * Q_BLOCK, :] for h in range(heads)], axis=1)


def forward_kernel(groups, me_ref, lengths_ref, *refs):
    pieces, outs = refs[:groups], refs[groups + 1 : 2 * groups + 1]
    o_ref, stats_ref, q_all, kv_all, attn_all = refs[2 * groups + 1 :]
    u = me_ref[0]
    length, qw = q_all.shape
    heads = qw // HEAD_DIM
    collect(u, pieces, (q_all, SCALE), (kv_all, None))
    starts = doc_starts(lengths_ref)
    for b in range(length // Q_BLOCK):
        here, there, bias = window(b, starts)
        keys, values = kv_all[there, :HEAD_DIM], kv_all[there, HEAD_DIM:]
        scores = nt(stacked(q_all, here, heads), keys)
        scores = scores + jnp.concatenate([bias] * heads, axis=0)
        peak = jnp.max(scores, axis=1, keepdims=True)
        weights = jnp.exp(scores - peak)
        inverse = 1.0 / jnp.sum(weights, axis=1, keepdims=True)
        mixed = side_by_side(nn((weights * inverse).astype(bf16), values), heads)
        o_ref[here, :] = mixed
        attn_all[here, :] = mixed.astype(bf16)
        stats_ref[here, :] = jnp.concatenate([side_by_side(peak, heads), side_by_side(inverse, heads)], axis=1)
    rows = length // groups
    for g in range(groups):
        hand_out(u, g, attn_all[g * rows : (g + 1) * rows, :], outs)


def backward_kernel(groups, me_ref, lengths_ref, cos_ref, sin_ref, o_ref, stats_ref, *refs):
    qkv_pieces, grad_pieces = refs[:groups], refs[groups : groups + groups // 2]
    q_all, kv_all, g_all, dq_all, acc = refs[-5:]
    outs = refs[-5 - groups : -5]
    u = me_ref[0]
    length, qw = q_all.shape
    heads = qw // HEAD_DIM
    collect(u, qkv_pieces, (q_all, SCALE), (kv_all, None))
    collect(u // 2, grad_pieces, (g_all, None))
    starts = doc_starts(lengths_ref)
    acc[...] = jnp.zeros_like(acc)
    for b in range(length // Q_BLOCK):
        here, there, bias = window(b, starts)
        keys, values = kv_all[there, :HEAD_DIM], kv_all[there, HEAD_DIM:]
        queries, grads = stacked(q_all, here, heads), stacked(g_all, here, heads)
        scores = nt(queries, keys) + jnp.concatenate([bias] * heads, axis=0)
        stats = stats_ref[here, :]
        peak, inverse = (
            jnp.concatenate([stats[:, i + h : i + h + 1] for h in range(heads)], axis=0) for i in (0, heads)
        )
        shares = jnp.exp(scores - peak) * inverse
        row_dot = jnp.sum(grads.astype(f32) * stacked(o_ref, here, heads), axis=1, keepdims=True)
        d_scores = (shares * (nt(grads, values) - row_dot)).astype(bf16)
        dq_all[here, :] = side_by_side(nn(d_scores, keys) * SCALE, heads)
        acc[:HEAD_DIM, there] += tn(queries, d_scores)
        acc[HEAD_DIM:, there] += tn(grads, shares.astype(bf16))
    rows = length // groups
    lower = lower_lanes(rows)
    value_lane = lax.broadcasted_iota(jnp.int32, (rows, 128), 1) >= HEAD_DIM
    for g in range(groups):
        here = slice(g * rows, (g + 1) * rows)
        cos, sin = cos_ref[here, :], sin_ref[here, :]
        parts = []
        for c in range(qw // 128):
            x = dq_all[here, c * 128 : (c + 1) * 128]
            parts.append(x * cos - turn(x, lower) * sin)
        x = acc[:, here].T
        parts.append(jnp.where(value_lane, x, x * cos - turn(x, lower) * sin))
        hand_out(u, g, jnp.concatenate(parts, axis=1).astype(bf16), outs)


def join_attn_kernel(groups, me_ref, *refs):
    u, out = me_ref[0], refs[-1]
    qw = QW // groups
    for j in range(groups):
        at = pl.multiple_of((u ^ j) * qw, qw)
        out[:, pl.ds(at, qw)] = refs[j][...]


def join_proj_kernel(groups, me_ref, *refs):
    u, (out, wide) = me_ref[0], refs[-2:]
    qw = QW // groups
    repeat = groups // KV_HEADS
    wide[...] = jnp.zeros_like(wide)
    for j in range(groups):
        at = pl.multiple_of((u ^ j) * qw, qw)
        out[:, pl.ds(at, qw)] = refs[j][:, :qw]
        back = refs[j][:, qw:].astype(f32)
        for kh in range(KV_HEADS):

            @pl.when((u ^ j) // repeat == kh)
            def _():
                wide[:, kh * 128 : (kh + 1) * 128] += back

    low = wide[...].astype(bf16)
    for at, half in ((QW, 0), (QW + KW, HEAD_DIM)):
        heads = [low[:, kh * 128 + half : kh * 128 + half + HEAD_DIM] for kh in range(KV_HEADS)]
        out[:, at : at + KW] = jnp.concatenate(heads, axis=1)


def tokens_kernel(slots, many, groups, factor, me_ref, tok_ref, d_out_ref, d_proj_ref, *refs):
    n = len(slots)
    d_tok_ref, d_gain_ref, wide, gains = refs[-4:]
    d = me_ref[1]
    width = tok_ref.shape[1]
    part = width // n
    d_proj = d_proj_ref[...]
    for j in range(n):
        at = pl.multiple_of((d ^ j) * part, part)
        w, ext = whole_slot(refs, slots[j], part)
        wide[:, pl.ds(at, part)] = nt(d_proj, w[:, : d_proj.shape[1]])
        gains[:, pl.ds(at, part)] = ext[part : part + 1, :part].astype(f32)
    x = tok_ref[...].astype(f32)
    inv = inverse_rms(x)
    unit = x * inv
    d_normed = wide[...]
    d_gain = jnp.sum(d_normed * unit, axis=0, keepdims=True) * factor
    scaled = d_normed * gains[...]
    mean = jnp.mean(scaled * unit, axis=1, keepdims=True)
    d_tok_ref[...] = (d_out_ref[...].astype(f32) + inv * (scaled - unit * mean)).astype(bf16)
    block = width // (groups * n)
    for e in range(n):
        starts = [g * (width // groups) + e * block for g in range(groups)]
        mine = jnp.concatenate([d_gain[:, s : s + block] for s in starts], axis=1)
        for g in range(groups):
            d_gain_ref[g, e : e + 1, :] = mine[:, g * block : (g + 1) * block]


def grads_kernel(slots, side, groups, factor, me_ref, slices, *refs):
    n = len(slots)
    outs, acc = refs[-1 - groups : -1], refs[-1]
    u, d = me_ref[0], me_ref[1]
    kept = acc.shape[0]
    for j in range(n):
        a = slices[d ^ j, side * kept : (side + 1) * kept, :]
        b, _ = whole_slot(refs, slots[j], a.shape[1])
        term = nn(a, b)
        if j == 0:
            acc[...] = term
        else:
            acc[...] += term
    block = kept // groups
    for g in range(groups):
        hand_out(u, g, acc[g * block : (g + 1) * block, :] * factor, outs)


def grads_and_pass_kernel(slots, side, groups, factor, me_ref, slices, *refs):
    refs, (pass_ref, *outs, pass_out, acc) = refs[: -3 - groups], refs[-3 - groups :]
    grads_kernel(slots, side, groups, factor, me_ref, slices, *refs, *outs, acc)
    pass_out[...] = pass_ref[...]


def weights_here(w_qkv, w_out, gain, me, qw):
    part, columns = w_qkv.shape
    sets = QW // qw // 2

    def kernel(me_ref, w_qkv_ref, w_out_ref, gain_ref, out):
        out[:part, :columns] = w_qkv_ref[...]
        for i in range(sets):
            at = pl.multiple_of((me_ref[0] ^ (2 * i)) * qw, qw)
            out[:part, columns + i * qw : columns + (i + 1) * qw] = w_out_ref[:, pl.ds(at, qw)]
        out[part:, :] = jnp.zeros_like(out[part:, :])
        out[part : part + 1, :part] = gain_ref[...]

    return pl.pallas_call(
        kernel,
        out_shape=shape(part + 16, columns + sets * qw),
        in_specs=[SMEM] + [VMEM] * 3,
        out_specs=VMEM,
        cost_estimate=about(2),
        name="weights_here",
    )(me, w_qkv, w_out, gain[None, :])


def after(value, *earlier):
    def kernel(*refs):
        del refs

    return pl.pallas_call(
        kernel,
        out_shape=shape(*value.shape),
        in_specs=[ANY] * (1 + len(earlier)),
        out_specs=ANY,
        input_output_aliases={0: 0},
        cost_estimate=about(0.1),
        name="after",
    )(value, *earlier)


def shape(*dims, dtype=bf16):
    return jax.ShapeDtypeStruct(dims, dtype)


def body(tokens, d_out, lengths, gain, w_qkv, w_out):
    groups, n = lax.axis_size("ulysses"), lax.axis_size("dp")
    u, d = lax.axis_index("ulysses"), lax.axis_index("dp")
    me = jnp.stack([u, d]).astype(jnp.int32)
    token_rows, grad_rows = tokens[0], d_out[0]
    rows, width = token_rows.shape
    length = rows * groups
    part = width // n
    heads = HEADS // groups
    qw = heads * HEAD_DIM
    columns = w_qkv.shape[1]
    factor = 1.0 / math.sqrt(length * n)
    block = width // (groups * n)
    kept = block * groups

    held = weights_here(w_qkv, w_out, gain, me, qw)
    held_near = neighbours(held, "dp")
    grad_pair = swap(grad_rows, "ulysses", 1)
    held_arrays, held_slots = complete(after(held, grad_pair), *held_near, "dp")

    bounds = jnp.cumsum(lengths[0]) - lengths[0]
    places = jnp.arange(length, dtype=jnp.int32)
    begins = jnp.max(jnp.where(bounds[None, :] <= places[:, None], bounds[None, :], 0), axis=1)
    places = places - begins
    inverse = ROPE_BASE ** (-jnp.arange(0, HEAD_DIM, 2).astype(f32) / HEAD_DIM)
    angles = places.astype(f32)[:, None] * jnp.tile(inverse, 4)[None, :]
    signs = jnp.where(jnp.arange(128) % HEAD_DIM < HEAD_DIM // 2, -1.0, 1.0).astype(f32)
    cos, sin = jnp.cos(angles), jnp.sin(angles) * signs[None, :]
    cos_here = lax.dynamic_slice_in_dim(cos, u * rows, rows)
    sin_here = lax.dynamic_slice_in_dim(sin, u * rows, rows)

    *pieces, normed = pl.pallas_call(
        functools.partial(proj_kernel, held_slots, len(held_arrays), groups),
        out_shape=[shape(rows, qw + 128)] * groups + [shape(rows, width)],
        in_specs=[SMEM] + [VMEM] * (3 + len(held_arrays)),
        out_specs=[VMEM] * (groups + 1),
        scratch_shapes=[pltpu.VMEM((rows, columns), f32)],
        compiler_params=params(56),
        cost_estimate=about(8),
        name="proj",
    )(me, token_rows, cos_here, sin_here, *held_arrays)
    qkv_here = [pieces[0]] + [swap(pieces[j], "ulysses", j) for j in range(1, groups)]

    own_slices = pl.pallas_call(
        functools.partial(slices_kernel, n, groups),
        out_shape=shape(n, 2 * kept, rows),
        in_specs=[VMEM] * 2,
        out_specs=VMEM,
        scratch_shapes=[pltpu.VMEM((width, rows), bf16)],
        compiler_params=params(56),
        cost_estimate=about(3),
        name="slices",
    )(normed, grad_rows)
    slices = lax.all_to_all(own_slices, "dp", 0, 0, tiled=True)
    sets = groups // 2
    pieces = pl.pallas_call(
        functools.partial(d_attn_kernel, held_slots, sets, columns),
        out_shape=[shape(2 * rows, qw)] * sets,
        in_specs=[SMEM] + [VMEM] * (2 + len(held_arrays)) + [ANY],
        out_specs=[VMEM] * sets,
        scratch_shapes=[pltpu.VMEM((width, sets * qw), bf16)],
        compiler_params=params(56),
        cost_estimate=about(6),
        name="d_attn",
    )(me, grad_rows, grad_pair, *held_arrays, qkv_here[1])
    grads_here = [pieces[0]] + [swap(after(pieces[i], *qkv_here[1:]), "ulysses", 2 * i) for i in range(1, sets)]

    *mixed, o, stats = pl.pallas_call(
        functools.partial(forward_kernel, groups),
        out_shape=[shape(rows, qw)] * groups
        + [shape(length, qw, dtype=f32), shape(length, 2 * heads, dtype=f32)],
        in_specs=[SMEM] * 2 + [VMEM] * groups + [ANY],
        out_specs=[VMEM] * (groups + 2),
        scratch_shapes=[
            pltpu.VMEM((length, qw), bf16),
            pltpu.VMEM((length, 128), bf16),
            pltpu.VMEM((length, qw), bf16),
        ],
        compiler_params=params(56),
        cost_estimate=about(10),
        name="forward",
    )(me, lengths[0], *qkv_here, own_slices)
    mixed = [mixed[0]] + [swap(mixed[j], "ulysses", j) for j in range(1, groups)]

    back = pl.pallas_call(
        functools.partial(backward_kernel, groups),
        out_shape=[shape(rows, qw + 128)] * groups,
        in_specs=[SMEM] * 2 + [VMEM] * (4 + groups + sets),
        out_specs=[VMEM] * groups,
        scratch_shapes=[
            pltpu.VMEM((length, qw), bf16),
            pltpu.VMEM((length, 128), bf16),
            pltpu.VMEM((length, qw), bf16),
            pltpu.VMEM((length, qw), f32),
            pltpu.VMEM((128, length), f32),
        ],
        compiler_params=params(56),
        cost_estimate=about(15),
        name="backward",
    )(me, lengths[0], cos, sin, o, stats, *qkv_here, *grads_here)
    back = [back[0]] + [swap(back[j], "ulysses", j) for j in range(1, groups)]

    attn = pl.pallas_call(
        functools.partial(join_attn_kernel, groups),
        out_shape=shape(rows, QW),
        in_specs=[SMEM] + [VMEM] * groups + [ANY] * 2,
        out_specs=VMEM,
        cost_estimate=about(2),
        name="join_attn",
    )(me, *mixed, slices, back[0])
    attn_near = neighbours(attn, "dp")

    d_proj = pl.pallas_call(
        functools.partial(join_proj_kernel, groups),
        out_shape=shape(rows, columns),
        in_specs=[SMEM] + [VMEM] * groups + [ANY] * 2,
        out_specs=VMEM,
        scratch_shapes=[pltpu.VMEM((rows, 128 * KV_HEADS), f32)],
        cost_estimate=about(3),
        name="join_proj",
    )(me, *back, *attn_near)
    proj_near = neighbours(d_proj, "dp")
    attn_arrays, attn_slots = complete(attn, *(after(a, d_proj) for a in attn_near), "dp")

    d_w_out, *terms = pl.pallas_call(
        functools.partial(grads_kernel, attn_slots, 1, groups, factor),
        out_shape=[shape(block, QW, dtype=f32)] * 2 + [shape(block, QW)] * (groups - 2),
        in_specs=[SMEM] + [VMEM] * (1 + len(attn_arrays)),
        out_specs=[VMEM] * groups,
        scratch_shapes=[pltpu.VMEM((kept, QW), f32)],
        compiler_params=params(56),
        cost_estimate=about(5),
        name="d_w_out",
    )(me, slices, *attn_arrays)

    out_terms = [swap(term, "ulysses", j) for j, term in enumerate(terms, 1)]

    d_tokens, partial_gain = pl.pallas_call(
        functools.partial(tokens_kernel, held_slots, len(held_arrays), groups, factor),
        out_shape=[shape(rows, width), shape(groups, n, block, dtype=f32)],
        in_specs=[SMEM] + [VMEM] * (3 + len(held_arrays)) + [ANY],
        out_specs=[VMEM] * 2,
        scratch_shapes=[pltpu.VMEM((rows, width), f32), pltpu.VMEM((1, width), f32)],
        compiler_params=params(56),
        cost_estimate=about(8),
        name="d_tokens",
    )(me, token_rows, grad_rows, d_proj, *held_arrays, d_w_out)

    proj_arrays, proj_slots = complete(after(d_proj, out_terms[0]), after(proj_near[0], partial_gain), proj_near[1], "dp")
    d_w_qkv, *terms, gain_terms = pl.pallas_call(
        functools.partial(grads_and_pass_kernel, proj_slots, 0, groups, factor),
        out_shape=[shape(block, columns, dtype=f32)] * 2 + [shape(block, columns)] * (groups - 2) + [shape(groups, n, block, dtype=f32)],
        in_specs=[SMEM] + [VMEM] * (1 + len(proj_arrays)) + [ANY] * (groups - 1) + [VMEM],
        out_specs=[VMEM] * (groups + 1),
        scratch_shapes=[pltpu.VMEM((kept, columns), f32)],
        compiler_params=params(56),
        cost_estimate=about(6),
        name="d_w_qkv",
    )(me, slices, *proj_arrays, *out_terms, partial_gain)
    for term in [swap(terms[j - 1], "ulysses", j) for j in reversed(range(1, groups))]:
        d_w_qkv = d_w_qkv + term.astype(f32)
    for term in out_terms:
        d_w_out = d_w_out + term.astype(f32)
    d_gain = gain_terms.reshape(groups * n, block)
    d_gain = lax.all_to_all(d_gain, ("ulysses", "dp"), 0, 0, tiled=True).sum(axis=0)
    return (d_tokens[None], d_w_qkv, d_w_out, d_gain)


def solution(mesh):
    in_specs = (
        P("dp", "ulysses", None),
        P("dp", "ulysses", None),
        P("dp", None),
        P("dp"),
        P("dp", None),
        P("dp", None),
    )
    out_specs = (
        P("dp", "ulysses", None),
        P(("ulysses", "dp"), None),
        P(("ulysses", "dp"), None),
        P(("ulysses", "dp")),
    )
    return jax.shard_map(body, mesh=mesh, in_specs=in_specs, out_specs=out_specs, check_vma=False)
```
